32 devices in a mesh: dp: 8 (over y, x, core), tensor: 4 (over z).
Axes of the slice: x: 2, y: 2, z: 4, core: 2. Of those that a mesh axis runs over, the one named last changes fastest.
Arguments:
- tokens: bfloat16 [8192, 768], P(('dp', 'tensor')), may hold values from -6 to 6
- gain_one: float32 [768], replicated, may hold values from 0.25 to 1.75
- shift_one: float32 [768], replicated, may hold values from -1.5 to 1.5
- qkv_weight: bfloat16 [768, 3, 768], P('dp', None, 'tensor'), may hold values from -0.3125 to 0.3125
- qkv_bias: float32 [3, 768], P(None, 'tensor'), may hold values from -1.5 to 1.5
- out_weight: bfloat16 [768, 768], P('tensor', 'dp'), may hold values from -0.875 to 0.875
- out_bias: float32 [768], replicated, may hold values from -1.5 to 1.5
- gain_two: float32 [768], replicated, may hold values from 0.25 to 1.75
- shift_two: float32 [768], replicated, may hold values from -1.5 to 1.5
- up_weight: bfloat16 [768, 3072], P('dp', 'tensor'), may hold values from -0.21875 to 0.21875
- up_bias: float32 [3072], P('tensor'), may hold values from -1.5 to 1.5
- down_weight: bfloat16 [3072, 768], P('tensor', 'dp'), may hold values from -0.15625 to 0.15625
- down_bias: float32 [768], replicated, may hold values from -1.5 to 1.5
- cotangent: bfloat16 [8192, 768], P(('dp', 'tensor')), may hold values from -6 to 6
Outputs:
- output: bfloat16 [8192, 768], P(('dp', 'tensor'))
- grad_tokens: float32 [8192, 768], P(('dp', 'tensor'))
- grad_gain_one: float32 [768], replicated
- grad_shift_one: float32 [768], replicated
- grad_qkv_weight: float32 [768, 3, 768], P('dp', None, 'tensor')
- grad_qkv_bias: float32 [3, 768], P(None, 'tensor')
- grad_out_weight: float32 [768, 768], P('tensor', 'dp')
- grad_out_bias: float32 [768], replicated
- grad_gain_two: float32 [768], replicated
- grad_shift_two: float32 [768], replicated
- grad_up_weight: float32 [768, 3072], P('dp', 'tensor')
- grad_up_bias: float32 [3072], P('tensor')
- grad_down_weight: float32 [3072, 768], P('tensor', 'dp')
- grad_down_bias: float32 [768], replicated
The draws below stay inside these ranges and needn't reach their ends.
All inputs are finite; a program needn't handle non-finite values.
Results may differ from the reference program's by a relative error of at most 0.018.
Values may be sent and summed in bfloat16 or wider, within the bound.
No kernel may reach another device: no remote copies, remote signals or barrier semaphores. Data moves between devices by JAX's collectives and lax.ppermute only.
A program may use at most 128 MiB of HBM per device.

```python
import jax
import jax.numpy as jnp
from jax import lax

D = 768
HEADS = 12
HEAD_DIM = 64
FF = 3072
SEQ_LEN = 1024
TOKENS = 8192
N_DP = 8


def level_of(stream_key, dims, pieces, low, largest):
    gain = 1.0
    for position, parts in pieces:
        heights = jax.random.uniform(jax.random.fold_in(jax.random.fold_in(stream_key, 6), position), (parts,), jnp.float32, low / len(pieces), largest / len(pieces))
        gain = gain * jnp.repeat(jnp.exp(heights), dims[position] // parts).reshape((-1,) + (1,) * (len(dims) - 1 - position))
    return gain


def noise(stream_key, shape, width, reach, cuts=(), held_as=jnp.bfloat16):
    entries = width * jax.random.normal(stream_key, shape, jnp.float32)
    if cuts:
        entries = entries * level_of(stream_key, shape, cuts, -0.22, 0.18)
    return jnp.clip(entries, -reach, reach).astype(held_as)


def setup_inputs(seed: int = 0) -> dict:
    splits = jax.random.split(jax.random.key(seed), 15)
    return {
        "tokens": noise(splits[0], (TOKENS, D), 1.0, 6.0, ((0, 32),)),
        "gain_one": jnp.clip(1.0 + 0.15 * jax.random.normal(splits[1], (D,), jnp.float32), 0.25, 1.75),
        "shift_one": noise(splits[2], (D,), 0.3, 1.5, (), jnp.float32),
        "qkv_weight": noise(splits[3], (D, 3, D), (D // 2) ** -0.5, 0.3125, ((0, 8), (2, 4))),
        "qkv_bias": noise(splits[4], (3, D), 0.3, 1.5, ((1, 4),), jnp.float32),
        "out_weight": noise(splits[5], (D, D), (D // 16) ** -0.5, 0.875, ((0, 4), (1, 8))),
        "out_bias": noise(splits[6], (D,), 0.3, 1.5, (), jnp.float32),
        "gain_two": jnp.clip(1.0 + 0.15 * jax.random.normal(splits[7], (D,), jnp.float32), 0.25, 1.75),
        "shift_two": noise(splits[8], (D,), 0.3, 1.5, (), jnp.float32),
        "up_weight": noise(splits[9], (D, FF), D ** -0.5, 0.21875, ((0, 8), (1, 4))),
        "up_bias": noise(splits[10], (FF,), 0.3, 1.5, ((0, 4),), jnp.float32),
        "down_weight": noise(splits[11], (FF, D), (FF // 2) ** -0.5, 0.15625, ((0, 4), (1, 8))),
        "down_bias": noise(splits[12], (D,), 0.3, 1.5, (), jnp.float32),
        "cotangent": noise(splits[13], (TOKENS, D), 1.0, 6.0, ((0, 32),)),
    }


EPS = 1e-05
HIGH = lax.Precision.HIGHEST

@jax.custom_vjp
def low(v):
    return lax.optimization_barrier(v.astype(jnp.bfloat16)).astype(jnp.float32)

@jax.custom_vjp
def low_back(v):
    return v

def low_keep(v):
    return (low(v), None)

def low_pass(kept, grad):
    return (grad,)

def back_keep(v):
    return (v, None)

def back_low(kept, grad):
    return (low(grad),)
low.defvjp(low_keep, low_pass)
low_back.defvjp(back_keep, back_low)

def layer_norm(values, ln_gain, ln_shift):
    middle = lax.optimization_barrier(jnp.mean(values, -1, keepdims=True))
    centred = values - middle
    variance = lax.optimization_barrier(jnp.mean(centred * centred, -1, keepdims=True))
    return centred * lax.rsqrt(variance + EPS) * ln_gain + ln_shift

def attention(queries, key_rows, value_rows):
    length = queries.shape[0]
    qblock = min(512, length)

    def one_block(block_index):
        first_row = block_index * qblock
        block_q = lax.dynamic_slice_in_dim(queries, first_row, qblock, 0)
        scores = jnp.einsum('qhd,khd->hqk', block_q, key_rows, precision=HIGH) * HEAD_DIM ** (-0.5)
        scores = low_back(scores)
        query_pos = first_row + lax.iota(jnp.int32, qblock)
        key_pos = lax.iota(jnp.int32, length)
        scores = jnp.where((key_pos[None, :] <= query_pos[:, None])[None], scores, -1e+30)
        row_max = lax.optimization_barrier(jnp.max(scores, -1, keepdims=True))
        weights = jnp.exp(scores - row_max)
        probabilities = weights / lax.optimization_barrier(jnp.sum(weights, -1, keepdims=True))
        return jnp.einsum('hqk,khd->qhd', low(probabilities), value_rows, precision=HIGH)
    blocks_out = lax.map(jax.checkpoint(one_block), jnp.arange(length // qblock, dtype=jnp.int32))
    return blocks_out.reshape(length, -1)

def forward(seq_tokens, gain_one, shift_one, qkv_weight, qkv_bias, out_weight, out_bias, gain_two, shift_two, up_weight, up_bias, down_weight, down_bias):
    length = seq_tokens.shape[0]
    normed = low(layer_norm(seq_tokens, gain_one, shift_one))
    mixed_rows = jnp.einsum('td,dcf->tcf', normed, qkv_weight, precision=HIGH) + qkv_bias
    mixed_rows = low_back(low(mixed_rows))
    head_rows = mixed_rows.reshape(length, 3, HEADS, HEAD_DIM)
    attended = attention(head_rows[:, 0], head_rows[:, 1], head_rows[:, 2])
    attended = low_back(low(attended))
    hidden_one = seq_tokens + low_back(jnp.dot(attended, out_weight, precision=HIGH)) + out_bias
    normed_two = low(layer_norm(hidden_one, gain_two, shift_two))
    up_value = low_back(jnp.dot(normed_two, up_weight, precision=HIGH) + up_bias)
    activated = low(jax.nn.gelu(up_value, approximate=False))
    return hidden_one + low_back(jnp.dot(activated, down_weight, precision=HIGH)) + down_bias

def reference(tokens, gain_one, shift_one, qkv_weight, qkv_bias, out_weight, out_bias, gain_two, shift_two, up_weight, up_bias, down_weight, down_bias, cotangent):
    weights = tuple((member.astype(jnp.float32) for member in (gain_one, shift_one, qkv_weight, qkv_bias, out_weight, out_bias, gain_two, shift_two, up_weight, up_bias, down_weight, down_bias)))
    sequences = tokens.astype(jnp.float32).reshape(N_DP, SEQ_LEN, D)
    grads_in = cotangent.astype(jnp.float32).reshape(N_DP, SEQ_LEN, D)

    def one_sequence(totals, seq_pair):
        seq_tokens, seq_grad = seq_pair
        result, pullback = jax.vjp(forward, seq_tokens, *weights)
        gradients = pullback(seq_grad)
        totals = jax.tree.map(jnp.add, totals, tuple(gradients[1:]))
        return (totals, (result.astype(jnp.bfloat16), gradients[0]))
    zero_totals = tuple((jnp.zeros_like(member) for member in weights))
    totals, (outputs, grad_rows) = lax.scan(one_sequence, zero_totals, (sequences, grads_in))
    grad_gain_one, grad_shift_one, grad_qkv_weight, grad_qkv_bias, grad_out_weight, grad_out_bias, grad_gain_two, grad_shift_two, grad_up_weight, grad_up_bias, grad_down_weight, grad_down_bias = totals
    return (outputs.reshape(TOKENS, D), grad_rows.reshape(TOKENS, D), grad_gain_one, grad_shift_one, grad_qkv_weight, grad_qkv_bias, grad_out_weight, grad_out_bias, grad_gain_two, grad_shift_two, grad_up_weight, grad_up_bias, grad_down_weight, grad_down_bias)
```

```python
import jax
import jax.numpy as jnp
from jax import lax
from jax.sharding import PartitionSpec as P

HEAD_DIM = 64
EPS = 1e-05
BF = jnp.bfloat16
F32 = jnp.float32
AXES = ("dp", "tensor")


def layer_norm(values, ln_gain, ln_shift):
    middle = jnp.mean(values, -1, keepdims=True)
    centred = values - middle
    variance = jnp.mean(centred * centred, -1, keepdims=True)
    return centred * lax.rsqrt(variance + EPS) * ln_gain + ln_shift


def exact_gelu(values):
    return jax.nn.gelu(values, approximate=False)


def dot_nn(left, right):
    return lax.dot_general(left, right, (((1,), (0,)), ((), ())), preferred_element_type=F32)


def dot_nt(left, right):
    return lax.dot_general(left, right, (((1,), (1,)), ((), ())), preferred_element_type=F32)


def dot_tn(left, right):
    return lax.dot_general(left, right, (((0,), (0,)), ((), ())), preferred_element_type=F32)


def block_scores(block_q, key_rows, first_row):
    qblock = block_q.shape[0]
    length = key_rows.shape[0]
    scores = jnp.einsum(
        "qhd,khd->hqk", block_q, key_rows, preferred_element_type=jnp.float32
    ) * HEAD_DIM ** (-0.5)
    query_pos = first_row + lax.iota(jnp.int32, qblock)
    key_pos = lax.iota(jnp.int32, length)
    return jnp.where((key_pos[None, :] <= query_pos[:, None])[None], scores, -1e30)


def attend(queries, key_rows, value_rows, qblock):
    length = queries.shape[0]

    def one_block(block_index):
        first_row = block_index * qblock
        block_q = lax.dynamic_slice_in_dim(queries, first_row, qblock, 0)
        scores = block_scores(block_q, key_rows, first_row)
        row_max = jnp.max(scores, -1, keepdims=True)
        weights = jnp.exp(scores - row_max)
        row_total = jnp.sum(weights, -1, keepdims=True)
        weights_low = (weights / row_total).astype(jnp.bfloat16)
        attended = jnp.einsum(
            "hqk,khd->qhd", weights_low, value_rows, preferred_element_type=jnp.float32
        )
        return (attended.astype(jnp.bfloat16), (row_max + jnp.log(row_total))[..., 0])

    blocks_out, log_totals = lax.map(one_block, jnp.arange(length // qblock, dtype=jnp.int32))
    return (blocks_out.reshape(length, -1), log_totals)


def attend_back(queries, key_rows, value_rows, grad_heads, log_totals, qblock):
    length = queries.shape[0]
    scale_factor = HEAD_DIM ** (-0.5)

    def one_block(running, block_index):
        grad_keys, grad_values = running
        first_row = block_index * qblock
        block_q = lax.dynamic_slice_in_dim(queries, first_row, qblock, 0)
        block_grad = lax.dynamic_slice_in_dim(grad_heads, first_row, qblock, 0)
        scores = block_scores(block_q, key_rows, first_row)
        weights = jnp.exp(scores - log_totals[block_index][..., None])
        weights_low = weights.astype(jnp.bfloat16)
        grad_values = grad_values + jnp.einsum(
            "hqk,qhd->khd", weights_low, block_grad, preferred_element_type=jnp.float32
        )
        grad_weights = jnp.einsum(
            "qhd,khd->hqk", block_grad, value_rows, preferred_element_type=jnp.float32
        )
        inner_sum = jnp.sum(weights * grad_weights, -1, keepdims=True)
        grad_scores = (weights * (grad_weights - inner_sum)).astype(jnp.bfloat16)
        grad_block_q = (
            jnp.einsum("hqk,khd->qhd", grad_scores, key_rows, preferred_element_type=jnp.float32)
            * scale_factor
        )
        grad_keys = (
            grad_keys
            + jnp.einsum("hqk,qhd->khd", grad_scores, block_q, preferred_element_type=jnp.float32)
            * scale_factor
        )
        return ((grad_keys, grad_values), grad_block_q)

    zero_rows = jnp.zeros(key_rows.shape, jnp.float32)
    (grad_keys, grad_values), grad_q_blocks = lax.scan(
        one_block, (zero_rows, zero_rows), jnp.arange(length // qblock, dtype=jnp.int32)
    )
    return (grad_q_blocks.reshape(queries.shape), grad_keys, grad_values)


class Plan:
    def __init__(self):
        self.n_dp = lax.axis_size("dp")
        self.n_t = lax.axis_size("tensor")
        assert self.n_t == 4 and self.n_dp % 2 == 0
        self.n_k = self.n_dp // 2
        assert self.n_k & (self.n_k - 1) == 0
        self.d = lax.axis_index("dp")
        self.t = lax.axis_index("tensor")
        self.k = self.d // 2
        self.c = self.d % 2
        self.h = self.t // 2
        self.r = jnp.where(self.c == self.h, self.t, self.t ^ 2)
        self.j = self.c + 2 * (self.t % 2)

    def send(self, value, where):
        pairs = []
        for d in range(self.n_dp):
            for t in range(self.n_t):
                to_d, to_t = where(d, t)
                pairs.append((d * self.n_t + t, to_d * self.n_t + to_t))
        return lax.ppermute(value, AXES, pairs)

    def swap_home(self, value):
        return self.send(value, lambda d, t: (d, t) if d % 2 == t // 2 else (d ^ 1, t ^ 2))

    def over_z(self, value):
        return self.send(value, lambda d, t: (d, t ^ 1))

    def over_core(self, value):
        return self.send(value, lambda d, t: (d ^ 1, t))

    def over_plane(self, value, p):
        return self.send(value, lambda d, t: (d ^ (2 * p), t))

    def group_gather(self, value):
        mine = jnp.stack([value, self.over_z(value)])
        return mine, self.over_core(mine)

    def group_sum(self, first, second):
        pair = first + self.over_core(second).astype(F32)
        return pair[0] + self.over_z(pair[1].astype(BF)).astype(F32)

    def spread(self, shard):
        got = []
        for i in (0, 1):
            got.append(
                self.send(
                    shard, lambda d, t, i=i: (2 * (d // 2) + t % 2, t // 2 + 2 * ((d % 2) ^ i))
                )
            )
        return got

    def to_slot(self, value):
        return self.send(value, lambda d, t: (2 * (d // 2) + t % 2, t // 2 + 2 * (d % 2)))

    def unspread(self, chunk):
        total = 0.0
        for i in (0, 1):
            part = lax.dynamic_index_in_dim(chunk, self.h ^ i, 0, keepdims=False)
            got = self.send(
                part, lambda d, t, i=i: (2 * (d // 2) + ((t // 2) ^ i), d % 2 + 2 * (t % 2))
            )
            total = total + got.astype(F32)
        return total

    def plane_gather(self, value):
        if self.n_k == 4:
            return jnp.stack([value] + [self.over_plane(value, p) for p in (1, 2, 3)])
        held = value[None]
        size = 1
        while size < self.n_k:
            held = jnp.concatenate([held, self.over_plane(held, size)])
            size *= 2
        return held

    def plane_sum(self, value):
        pick = lambda p: lax.dynamic_index_in_dim(value, self.k ^ p, 0, keepdims=False)
        if self.n_k == 4:
            total = pick(0).astype(F32)
            for p in (1, 2, 3):
                total = total + self.over_plane(pick(p).astype(BF), p).astype(F32)
            return total
        held = jnp.stack([pick(p) for p in range(self.n_k)]).astype(F32)
        size = self.n_k // 2
        while size:
            held = held[:size] + self.over_plane(held[size:].astype(BF), size).astype(F32)
            size //= 2
        return held[0]

    def ordered_weight(self, held):
        flat = held.reshape((self.n_dp,) + held.shape[2:])
        parts = []
        for d in range(self.n_dp):
            at = ((d // 2) ^ self.k) * 2 + ((d % 2) ^ self.h)
            parts.append(lax.dynamic_index_in_dim(flat, at, 0, keepdims=False))
        return jnp.concatenate(parts, 0)

    def ordered_rows(self, first, second):
        flat = jnp.concatenate([first, second])
        return jnp.concatenate(
            [lax.dynamic_index_in_dim(flat, a ^ self.r, 0, keepdims=False) for a in range(4)], 0
        )

    def relative_rows(self, value):
        rows = value.reshape((4, -1) + value.shape[1:])
        return [lax.dynamic_index_in_dim(rows, i ^ self.r, 0, keepdims=False) for i in range(4)]

    def all_sum(self, value):
        value = value + self.over_core(value)
        p = 1
        while p < self.n_k:
            value = value + self.over_plane(value, p)
            p *= 2
        value = value + self.over_z(value)
        return value + self.send(value, lambda d, t: (d, t ^ 2))


def after(value, *earlier):
    return lax.optimization_barrier((value,) + earlier)[0]


def local(
    tokens,
    gain_one,
    shift_one,
    qkv_weight,
    qkv_bias,
    out_weight,
    out_bias,
    gain_two,
    shift_two,
    up_weight,
    up_bias,
    down_weight,
    down_bias,
    cotangent,
):
    plan = Plan()
    rows, width = tokens.shape
    shard = qkv_weight.shape[0]
    heads_wide = qkv_weight.shape[2]
    units = up_weight.shape[1]
    n_heads = heads_wide // HEAD_DIM
    length = 4 * rows
    n_dp, n_k = plan.n_dp, plan.n_k

    x_own = plan.swap_home(tokens)
    attn_shard = jnp.concatenate([qkv_weight.reshape(shard, 3 * heads_wide), out_weight.T], 1)
    attn_spread = jnp.stack(plan.spread(attn_shard))
    biases = plan.to_slot(jnp.concatenate([qkv_bias.reshape(-1), up_bias]))
    qkv_bias_j, up_bias_j = biases[: 3 * heads_wide], biases[3 * heads_wide :]
    x_first, x_second = plan.group_gather(x_own)
    attn_full = plan.ordered_weight(plan.plane_gather(attn_spread))
    qkv_flat, out_t = attn_full[:, : 3 * heads_wide], attn_full[:, 3 * heads_wide :]

    mlp_shard = after(jnp.concatenate([up_weight, down_weight.T], 1), attn_spread)
    mlp_spread = jnp.stack(plan.spread(mlp_shard))
    g_own = plan.swap_home(after(cotangent, x_second))
    g_first, g_second = plan.group_gather(g_own)
    mlp_full = plan.ordered_weight(plan.plane_gather(after(mlp_spread, attn_full)))
    up_j, down_tj = mlp_full[:, :units], mlp_full[:, units:]
    out_first, out_second = plan.group_gather(out_t)

    x_all = plan.ordered_rows(x_first, x_second).astype(F32)
    normed = layer_norm(x_all, gain_one, shift_one).astype(BF)
    mixed = (dot_nn(normed, qkv_flat) + qkv_bias_j).astype(BF)
    mixed = mixed.reshape(length, 3, n_heads, HEAD_DIM)
    queries, key_rows, value_rows = mixed[:, 0], mixed[:, 1], mixed[:, 2]
    qblock = min(512, length)
    attended, log_totals = attend(queries, key_rows, value_rows, qblock)
    att_first, att_second = plan.group_gather(attended)
    proj = (
        dot_nt(att_first[0], out_first[0])
        + dot_nt(att_first[1], out_first[1])
        + dot_nt(att_second[0], out_second[0])
        + dot_nt(att_second[1], out_second[1])
    )
    x_rel = jnp.concatenate([x_first, x_second]).reshape(length, width).astype(F32)
    hidden = x_rel + jnp.concatenate(plan.relative_rows(proj)) + out_bias
    normed_two = layer_norm(hidden, gain_two, shift_two).astype(BF)
    hidden_own = hidden[:rows]

    g_all = jnp.concatenate([g_first, g_second]).reshape(length, width)
    up_value = dot_nn(normed_two, up_j) + up_bias_j
    activated, gelu_back = jax.vjp(exact_gelu, up_value)
    act = activated.astype(BF)
    grad_up = gelu_back(dot_nn(g_all, down_tj))[0].astype(BF)
    gn2 = dot_nt(grad_up, up_j).reshape(4, rows, width)
    gn2_own = plan.group_sum(gn2[:2], gn2[2:].astype(BF))
    up_bias_grad = jnp.sum(grad_up.astype(F32), 0)
    up_grad = dot_tn(normed_two, grad_up)
    down_grad_t = dot_tn(g_all, act)
    mlp_out = dot_nt(act, down_tj).reshape(4, rows, width)
    mlp_own = plan.group_sum(mlp_out[:2], mlp_out[2:].astype(BF))
    output = plan.swap_home((hidden_own + mlp_own + down_bias).astype(BF))

    mlp_grad = jnp.concatenate([up_grad, down_grad_t], 1).reshape(n_k, 2, shard, 2 * units)
    mlp_summed = plan.unspread(plan.plane_sum(mlp_grad).astype(BF))

    norm_two_back = jax.vjp(layer_norm, hidden_own, gain_two, shift_two)[1]
    grad_from_norm, gain_two_grad, shift_two_grad = norm_two_back(gn2_own)
    g_own32 = g_own.astype(F32)
    grad_hidden = g_own32 + grad_from_norm
    out_bias_grad = jnp.sum(grad_hidden, 0)
    down_bias_grad = jnp.sum(g_own32, 0)
    gh_first, gh_second = plan.group_gather(grad_hidden.astype(BF))
    gh_all = plan.ordered_rows(gh_first, gh_second)

    grad_att = dot_nn(gh_all, out_t).astype(BF).reshape(length, n_heads, HEAD_DIM)
    grad_q, grad_k, grad_v = attend_back(
        queries, key_rows, value_rows, grad_att, log_totals, qblock
    )
    grad_mixed = jnp.stack([grad_q, grad_k, grad_v], 1).astype(BF).reshape(length, 3 * heads_wide)
    qkv_bias_grad = jnp.sum(grad_mixed.astype(F32), 0).reshape(3, heads_wide)
    gn1 = jnp.stack(plan.relative_rows(dot_nt(grad_mixed, qkv_flat)))
    gn1_own = plan.group_sum(gn1[:2], gn1[2:].astype(BF))
    norm_one_back = jax.vjp(layer_norm, x_own.astype(F32), gain_one, shift_one)[1]
    grad_stream, gain_one_grad, shift_one_grad = norm_one_back(gn1_own)
    grad_tokens = plan.swap_home((grad_hidden + grad_stream).astype(BF)).astype(F32)

    out_grad_t = dot_tn(gh_all, attended)
    qkv_grad = dot_tn(normed, grad_mixed)
    attn_grad = jnp.concatenate([qkv_grad, out_grad_t], 1)
    attn_grad = attn_grad.reshape(n_k, 2, shard, 4 * heads_wide)
    attn_summed = plan.unspread(plan.plane_sum(attn_grad).astype(BF))

    qkv_bias_full = lax.dynamic_update_slice_in_dim(
        jnp.zeros((3, width), F32), qkv_bias_grad, plan.j * heads_wide, 1
    )
    up_bias_full = lax.dynamic_update_slice_in_dim(
        jnp.zeros((4 * units,), F32), up_bias_grad, plan.j * units, 0
    )
    small = jnp.concatenate(
        [
            gain_one_grad,
            shift_one_grad,
            out_bias_grad,
            gain_two_grad,
            shift_two_grad,
            down_bias_grad,
            qkv_bias_full.reshape(-1),
            up_bias_full,
        ]
    )
    small = plan.all_sum(small)
    vec = [small[i * width : (i + 1) * width] for i in range(6)]
    qkv_bias_summed = lax.dynamic_slice_in_dim(
        small[6 * width : 9 * width].reshape(3, width), plan.t * heads_wide, heads_wide, 1
    )
    up_bias_summed = lax.dynamic_slice_in_dim(small[9 * width :], plan.t * units, units, 0)
    return (
        output,
        grad_tokens,
        vec[0],
        vec[1],
        attn_summed[:, : 3 * heads_wide].reshape(shard, 3, heads_wide),
        qkv_bias_summed,
        attn_summed[:, 3 * heads_wide :].T,
        vec[2],
        vec[3],
        vec[4],
        mlp_summed[:, :units],
        up_bias_summed,
        mlp_summed[:, units:].T,
        vec[5],
    )


def solution(mesh):
    in_specs = (
        P(("dp", "tensor"), None),
        P(),
        P(),
        P("dp", None, "tensor"),
        P(None, "tensor"),
        P("tensor", "dp"),
        P(),
        P(),
        P(),
        P("dp", "tensor"),
        P("tensor"),
        P("tensor", "dp"),
        P(),
        P(("dp", "tensor"), None),
    )
    out_specs = (
        P(("dp", "tensor"), None),
        P(("dp", "tensor"), None),
        P(),
        P(),
        P("dp", None, "tensor"),
        P(None, "tensor"),
        P("tensor", "dp"),
        P(),
        P(),
        P(),
        P("dp", "tensor"),
        P("tensor"),
        P("tensor", "dp"),
        P(),
    )
    return jax.shard_map(local, mesh=mesh, in_specs=in_specs, out_specs=out_specs, check_vma=False)
```

```python
import jax
import jax.numpy as jnp
from jax import lax
from jax.experimental import pallas as pl
from jax.experimental.pallas import tpu as pltpu
from jax.sharding import PartitionSpec as P

HEAD_DIM = 64
EPS = 1e-05
BF = jnp.bfloat16
F32 = jnp.float32
AXES = ("dp", "tensor")


def dot_nn(left, right):
    return lax.dot_general(left, right, (((1,), (0,)), ((), ())), preferred_element_type=F32)


def dot_nt(left, right):
    return lax.dot_general(left, right, (((1,), (1,)), ((), ())), preferred_element_type=F32)


def dot_tn(left, right):
    return lax.dot_general(left, right, (((0,), (0,)), ((), ())), preferred_element_type=F32)


class Plan:
    def __init__(self):
        self.n_dp = lax.axis_size("dp")
        self.n_t = lax.axis_size("tensor")
        assert self.n_t == 4 and self.n_dp % 2 == 0
        self.n_k = self.n_dp // 2
        assert self.n_k & (self.n_k - 1) == 0
        self.d = lax.axis_index("dp")
        self.t = lax.axis_index("tensor")
        self.k = self.d // 2
        self.c = self.d % 2
        self.h = self.t // 2
        self.r = jnp.where(self.c == self.h, self.t, self.t ^ 2)
        self.j = self.c + 2 * (self.t % 2)

    def send(self, value, where):
        pairs = []
        for d in range(self.n_dp):
            for t in range(self.n_t):
                to_d, to_t = where(d, t)
                pairs.append((d * self.n_t + t, to_d * self.n_t + to_t))
        return lax.ppermute(value, AXES, pairs)

    def swap_home(self, value):
        return self.send(value, lambda d, t: (d, t) if d % 2 == t // 2 else (d ^ 1, t ^ 2))

    def over_z(self, value):
        return self.send(value, lambda d, t: (d, t ^ 1))

    def over_core(self, value):
        return self.send(value, lambda d, t: (d ^ 1, t))

    def over_plane(self, value, p):
        return self.send(value, lambda d, t: (d ^ (2 * p), t))

    def group_gather(self, value):
        mine = jnp.stack([value, self.over_z(value)])
        return mine, self.over_core(mine)

    def group_sum(self, first, second):
        pair = first + self.over_core(second).astype(F32)
        return pair[0] + self.over_z(pair[1].astype(BF)).astype(F32)

    def spread(self, shard):
        got = []
        for i in (0, 1):
            got.append(
                self.send(
                    shard, lambda d, t, i=i: (2 * (d // 2) + t % 2, t // 2 + 2 * ((d % 2) ^ i))
                )
            )
        return got

    def to_slot(self, value):
        return self.send(value, lambda d, t: (2 * (d // 2) + t % 2, t // 2 + 2 * (d % 2)))

    def unspread(self, chunk):
        total = 0.0
        for i in (0, 1):
            part = lax.dynamic_index_in_dim(chunk, self.h ^ i, 0, keepdims=False)
            got = self.send(
                part, lambda d, t, i=i: (2 * (d // 2) + ((t // 2) ^ i), d % 2 + 2 * (t % 2))
            )
            total = total + got.astype(F32)
        return total

    def plane_gather(self, value):
        if self.n_k == 4:
            return jnp.stack([value] + [self.over_plane(value, p) for p in (1, 2, 3)])
        held = value[None]
        size = 1
        while size < self.n_k:
            held = jnp.concatenate([held, self.over_plane(held, size)])
            size *= 2
        return held

    def plane_sum(self, value):
        pick = lambda p: lax.dynamic_index_in_dim(value, self.k ^ p, 0, keepdims=False)
        if self.n_k == 4:
            total = pick(0).astype(F32)
            for p in (1, 2, 3):
                total = total + self.over_plane(pick(p).astype(BF), p).astype(F32)
            return total
        held = jnp.stack([pick(p) for p in range(self.n_k)]).astype(F32)
        size = self.n_k // 2
        while size:
            held = held[:size] + self.over_plane(held[size:].astype(BF), size).astype(F32)
            size //= 2
        return held[0]

    def ordered_weight(self, held):
        flat = held.reshape((self.n_dp,) + held.shape[2:])
        parts = []
        for d in range(self.n_dp):
            at = ((d // 2) ^ self.k) * 2 + ((d % 2) ^ self.h)
            parts.append(lax.dynamic_index_in_dim(flat, at, 0, keepdims=False))
        return jnp.concatenate(parts, 0)

    def ordered_rows(self, first, second):
        flat = jnp.concatenate([first, second])
        return jnp.concatenate(
            [lax.dynamic_index_in_dim(flat, a ^ self.r, 0, keepdims=False) for a in range(4)], 0
        )

    def relative_rows(self, value):
        rows = value.reshape((4, -1) + value.shape[1:])
        return [lax.dynamic_index_in_dim(rows, i ^ self.r, 0, keepdims=False) for i in range(4)]

    def all_sum(self, value):
        value = value + self.over_core(value)
        p = 1
        while p < self.n_k:
            value = value + self.over_plane(value, p)
            p *= 2
        value = value + self.over_z(value)
        return value + self.send(value, lambda d, t: (d, t ^ 2))


def after(value, *earlier):
    return lax.optimization_barrier((value,) + earlier)[0]


def call(body, outs, args, flops, scratch=()):
    shapes = tuple(jax.ShapeDtypeStruct(shape, dtype) for shape, dtype in outs)
    moved = sum(a.size * a.dtype.itemsize for a in args)
    moved += sum(s.size * s.dtype.itemsize for s in shapes)
    return pl.pallas_call(
        body,
        out_shape=shapes,
        in_specs=[pl.BlockSpec(memory_space=pltpu.SMEM)]
        + [pl.BlockSpec(memory_space=pltpu.VMEM)] * (len(args) - 1),
        out_specs=tuple(pl.BlockSpec(memory_space=pltpu.VMEM) for _ in shapes),
        scratch_shapes=list(scratch),
        compiler_params=pltpu.CompilerParams(vmem_limit_bytes=50 * 2**20),
        cost_estimate=pl.CostEstimate(flops=flops, bytes_accessed=moved, transcendentals=0),
    )(*args)


def normalise(values):
    middle = jnp.mean(values, -1, keepdims=True)
    centred = values - middle
    variance = jnp.mean(centred * centred, -1, keepdims=True)
    rate = lax.rsqrt(variance + EPS)
    return centred * rate, rate


def norm_back(grad, hat, rate, gain):
    scaled = grad * gain
    first = jnp.mean(scaled, -1, keepdims=True)
    second = jnp.mean(scaled * hat, -1, keepdims=True)
    return rate * (scaled - first - hat * second)


def col_sum(values):
    return jnp.sum(values, 0, keepdims=True)


def chunk_at(ids, i, rows):
    return pl.ds(pl.multiple_of((ids[2] ^ i) * rows, rows), rows)


def order_weight(ids, pieces, scratch, shard):
    if len(pieces) == 1:
        scratch[...] = pieces[0][0]
        return
    for p, piece in enumerate(pieces):
        for i in range(2):
            at = 2 * (ids[0] ^ p) + (ids[1] ^ i)
            scratch[pl.ds(pl.multiple_of(at * shard, shard), shard), :] = piece[i]


def mixed_kernel(n_w, shard, ids, x0, x1, x2, x3, gain, shift, bias, *refs):
    pieces, (normed, mixed, w_all) = refs[:n_w], refs[n_w:]
    order_weight(ids, pieces, w_all, shard)
    wide = mixed.shape[1]
    for i, x in enumerate((x0, x1, x2, x3)):
        rows = x.shape[0]
        hat, _ = normalise(x[...].astype(F32))
        low = (hat * gain[...] + shift[...]).astype(BF)
        normed[chunk_at(ids, i, rows), :] = low
        out = dot_nn(low, w_all[:, :wide]) + bias[...]
        mixed[chunk_at(ids, i, rows), :] = out.astype(BF)


def attend_kernel(ids, mixed, attended, logs):
    length, wide = attended.shape
    block = min(256, length)
    tri = lax.broadcasted_iota(jnp.int32, (block, block), 0) <= lax.broadcasted_iota(
        jnp.int32, (block, block), 1
    )
    for head in range(wide // HEAD_DIM):
        at = head * HEAD_DIM
        q_t = (mixed[:, at : at + HEAD_DIM].astype(F32) * HEAD_DIM ** (-0.5)).T.astype(BF)
        keys = mixed[:, wide + at : wide + at + HEAD_DIM]
        v_t = mixed[:, 2 * wide + at : 2 * wide + at + HEAD_DIM].astype(F32).T.astype(BF)
        for b in range(length // block):
            low = b * block
            q_b = q_t[:, low : low + block]
            near = jnp.where(tri, dot_nn(keys[low : low + block], q_b), -1e30)
            top = jnp.max(near, 0, keepdims=True)
            if b:
                far = dot_nn(keys[:low], q_b)
                top = jnp.maximum(top, jnp.max(far, 0, keepdims=True))
            near = jnp.exp(near - top)
            total = col_sum(near)
            out = dot_nn(v_t[:, low : low + block], near.astype(BF))
            if b:
                far = jnp.exp(far - top)
                total = total + col_sum(far)
                out = out + dot_nn(v_t[:, :low], far.astype(BF))
            out = out * (1.0 / total)
            attended[low : low + block, at : at + HEAD_DIM] = out.T.astype(BF)
            logs[head : head + 1, low : low + block] = top + jnp.log(total)


def middle_kernel(n_w, shard, ids, *refs):
    att, outs, xs, gs = refs[0:4], refs[4 : 4 + 4], refs[8:12], refs[12:16]
    out_bias, gain, shift, up_bias = refs[16:20]
    pieces = refs[20 : 20 + n_w]
    (hidden_own, normed_two, act, grad_up, first, second, up_bias_grad, down_t) = refs[
        20 + n_w : 28 + n_w
    ]
    out_w, up_w, both = refs[28 + n_w :]
    wide = att[0].shape[1]
    units = act.shape[1]
    order_weight(ids, pieces, both, shard)
    up_w[...] = both[:, :units]
    down_t[...] = both[:, units:]
    for g, out in enumerate(outs):
        if n_w == 1:
            out_w[g] = out[0, 0]
        else:
            for p in range(n_w):
                for i in range(2):
                    at = 2 * (ids[0] ^ p) + (ids[1] ^ i)
                    out_w[g, pl.ds(pl.multiple_of(at * shard, shard), shard), :] = out[p, i]
    bias_sum = jnp.zeros((1, units), F32)
    for i in range(4):
        rows = xs[0].shape[0]
        hidden = xs[i][...].astype(F32) + out_bias[...]
        for g in range(4):
            hidden = hidden + dot_nt(att[g][chunk_at(ids, i, rows), :], out_w[g])
        if i == 0:
            hidden_own[...] = hidden
        hat, _ = normalise(hidden)
        low = (hat * gain[...] + shift[...]).astype(BF)
        span = slice(i * rows, (i + 1) * rows)
        normed_two[span, :] = low
        up = dot_nn(low, up_w[...]) + up_bias[...]
        whole = 0.5 * (1.0 + lax.erf(up * 0.5**0.5))
        act[span, :] = (up * whole).astype(BF)
        slope = whole + up * (jnp.exp(-0.5 * up * up) * (2.0 * jnp.pi) ** (-0.5))
        grad = (dot_nn(gs[i][...], down_t[...]) * slope).astype(BF)
        grad_up[span, :] = grad
        bias_sum = bias_sum + col_sum(grad.astype(F32))
        back = dot_nt(grad, up_w[...])
        if i < 2:
            first[i] = back
        else:
            second[i - 2] = back.astype(BF)
    up_bias_grad[...] = bias_sum


def mlp_grad_kernel(n_o, shard, ids, normed_two, g0, g1, g2, g3, act, grad_up, *refs):
    outs, scratch = refs[:n_o], refs[n_o]
    units = act.shape[1]
    rows = g0.shape[0]
    scratch[:, :units] = dot_tn(normed_two[...], grad_up[...])
    total = 0.0
    for i, g in enumerate((g0, g1, g2, g3)):
        total = total + dot_tn(g[...], act[i * rows : (i + 1) * rows, :])
    scratch[:, units:] = total
    emit_grad(ids, scratch, outs, shard)


def emit_grad(ids, scratch, outs, shard):
    if len(outs) == 1:
        outs[0][...] = scratch[...]
        return
    for p, out in enumerate(outs):
        at = pl.ds(pl.multiple_of((ids[0] ^ p) * 2 * shard, 2 * shard), 2 * shard)
        out[...] = scratch[at, :].astype(out.dtype)


def mlp_out_kernel(ids, act, down_t, first, second):
    rows = first.shape[1]
    for i in range(4):
        out = dot_nt(act[i * rows : (i + 1) * rows, :], down_t[...])
        if i < 2:
            first[i] = out
        else:
            second[i - 2] = out.astype(BF)


def norm_two_kernel(ids, own, got_core, got_z, hidden, g, gain, grad_hidden, low, sums):
    grad = own[...] + got_core[...].astype(F32) + got_z[...].astype(F32)
    hat, rate = normalise(hidden[...])
    g32 = g[...].astype(F32)
    total = g32 + norm_back(grad, hat, rate, gain[...])
    grad_hidden[...] = total
    low[...] = total.astype(BF)
    sums[0:1, :] = col_sum(total)
    sums[1:2, :] = col_sum(grad * hat)
    sums[2:3, :] = col_sum(grad)
    sums[3:4, :] = col_sum(g32)


def norm_one_kernel(ids, own, got_core, got_z, x, gain, grad_hidden, out):
    grad = own[...] + got_core[...].astype(F32) + got_z[...].astype(F32)
    hat, rate = normalise(x[...].astype(F32))
    total = grad_hidden[...] + norm_back(grad, hat, rate, gain[...])
    out[...] = total.astype(BF)


def attend_back_kernel(ids, mixed, logs, w_all, gh0, gh1, gh2, gh3, x0, x1, x2, x3, *refs):
    grad_mixed, first, second, bias_grad, sums, g_rows, gm32 = refs
    length, wide3 = mixed.shape
    wide = wide3 // 3
    rows = x0.shape[0]
    block = min(256, length)
    for i, gh in enumerate((gh0, gh1, gh2, gh3)):
        g_rows[chunk_at(ids, i, rows), :] = dot_nn(gh[...], w_all[:, wide3:])
    tri = lax.broadcasted_iota(jnp.int32, (block, block), 0) <= lax.broadcasted_iota(
        jnp.int32, (block, block), 1
    )
    for head in range(wide // HEAD_DIM):
        at = head * HEAD_DIM
        scaled = mixed[:, at : at + HEAD_DIM].astype(F32) * HEAD_DIM ** (-0.5)
        q_rows = scaled.astype(BF)
        q_t = scaled.T.astype(BF)
        keys = mixed[:, wide + at : wide + at + HEAD_DIM]
        k_t = keys.astype(F32).T.astype(BF)
        values = mixed[:, 2 * wide + at : 2 * wide + at + HEAD_DIM]
        grad32 = g_rows[:, at : at + HEAD_DIM]
        grad_rows = grad32.astype(BF)
        grad_t = grad32.T.astype(BF)
        for b in range(length // block):
            low, end = b * block, (b + 1) * block
            q_b = q_t[:, low:end]
            g_b = grad_t[:, low:end]
            log = logs[head : head + 1, low:end]
            near = jnp.where(tri, jnp.exp(dot_nn(keys[low:end], q_b) - log), 0.0)
            near_d = dot_nn(values[low:end], g_b)
            inner = col_sum(near * near_d)
            if b:
                far = jnp.exp(dot_nn(keys[:low], q_b) - log)
                far_d = dot_nn(values[:low], g_b)
                inner = inner + col_sum(far * far_d)
            near_s = (near * (near_d - inner)).astype(BF)
            grad_q = dot_nn(k_t[:, low:end], near_s)
            gm32[low:end, HEAD_DIM : 2 * HEAD_DIM] = dot_nn(near_s, q_rows[low:end])
            gm32[low:end, 2 * HEAD_DIM :] = dot_nn(near.astype(BF), grad_rows[low:end])
            if b:
                far_s = (far * (far_d - inner)).astype(BF)
                grad_q = grad_q + dot_nn(k_t[:, :low], far_s)
                gm32[:low, HEAD_DIM : 2 * HEAD_DIM] += dot_nn(far_s, q_rows[low:end])
                gm32[:low, 2 * HEAD_DIM :] += dot_nn(far.astype(BF), grad_rows[low:end])
            gm32[low:end, :HEAD_DIM] = grad_q.T * HEAD_DIM ** (-0.5)
        for part in range(3):
            grad_mixed[:, part * wide + at : part * wide + at + HEAD_DIM] = gm32[
                :, part * HEAD_DIM : (part + 1) * HEAD_DIM
            ].astype(BF)
    bias_grad[...] = col_sum(grad_mixed[...].astype(F32))
    gain_sum = jnp.zeros((1, x0.shape[1]), F32)
    shift_sum = gain_sum
    for i, x in enumerate((x0, x1, x2, x3)):
        back = dot_nt(grad_mixed[chunk_at(ids, i, rows), :], w_all[:, :wide3])
        hat, _ = normalise(x[...].astype(F32))
        gain_sum = gain_sum + col_sum(back * hat)
        shift_sum = shift_sum + col_sum(back)
        if i < 2:
            first[i] = back
        else:
            second[i - 2] = back.astype(BF)
    sums[0:1, :] = gain_sum
    sums[1:2, :] = shift_sum


def attn_grad_kernel(n_o, shard, ids, normed, grad_mixed, gh0, gh1, gh2, gh3, attended, *refs):
    outs, scratch = refs[:n_o], refs[n_o]
    wide3 = grad_mixed.shape[1]
    rows = gh0.shape[0]
    scratch[:, :wide3] = dot_tn(normed[...], grad_mixed[...])
    total = 0.0
    for i, gh in enumerate((gh0, gh1, gh2, gh3)):
        total = total + dot_tn(gh[...], attended[chunk_at(ids, i, rows), :])
    scratch[:, wide3:] = total
    emit_grad(ids, scratch, outs, shard)


def local(
    tokens,
    gain_one,
    shift_one,
    qkv_weight,
    qkv_bias,
    out_weight,
    out_bias,
    gain_two,
    shift_two,
    up_weight,
    up_bias,
    down_weight,
    down_bias,
    cotangent,
):
    plan = Plan()
    rows, width = tokens.shape
    shard = qkv_weight.shape[0]
    wide = qkv_weight.shape[2]
    wide3 = 3 * wide
    units = up_weight.shape[1]
    length = 4 * rows
    n_k = plan.n_k
    direct = n_k == 4 and shard % 16 == 0
    n_w = n_k if direct else 1
    n_o = n_k if direct else 1
    ids = jnp.stack([plan.k, plan.h, plan.r]).astype(jnp.int32)
    row = lambda v: v.reshape(1, -1)
    row_gain_one, row_shift_one = row(gain_one), row(shift_one)
    row_gain_two, row_shift_two = row(gain_two), row(shift_two)

    def plane_pieces(value):
        if direct:
            return [value] + [plan.over_plane(value, p) for p in (1, 2, 3)]
        return [plan.ordered_weight(plan.plane_gather(value))[None]]

    def plane_total(pieces):
        if direct:
            total = pieces[0]
            for p in (1, 2, 3):
                total = total + plan.over_plane(pieces[p], p).astype(F32)
            return total
        return plan.plane_sum(pieces[0].reshape((n_k, 2 * shard) + pieces[0].shape[1:]))

    def grad_outs(n):
        if direct:
            return [((2 * shard, n), F32)] + [((2 * shard, n), BF)] * (n_k - 1)
        return [((width, n), F32)]

    x0 = plan.swap_home(tokens)
    attn_shard = jnp.concatenate([qkv_weight.reshape(shard, wide3), out_weight.T], 1)
    attn_spread = jnp.stack(plan.spread(attn_shard))
    biases = plan.to_slot(jnp.concatenate([qkv_bias.reshape(-1), up_bias]))
    qkv_bias_j, up_bias_j = row(biases[:wide3]), row(biases[wide3:])
    x1 = plan.over_z(x0)
    x2 = plan.over_core(x0)
    x3 = plan.over_core(x1)
    attn_w = plane_pieces(attn_spread)
    normed, mixed, w_all = call(
        lambda *refs: mixed_kernel(n_w, shard, *refs),
        [((length, width), BF), ((length, wide3), BF), ((width, width), BF)],
        [ids, x0, x1, x2, x3, row_gain_one, row_shift_one, qkv_bias_j] + attn_w,
        2 * length * width * wide3,
    )

    mlp_shard = after(jnp.concatenate([up_weight, down_weight.T], 1), attn_spread)
    mlp_spread = jnp.stack(plan.spread(mlp_shard))
    mlp_w = plane_pieces(after(mlp_spread, mixed))
    out_t = jnp.stack([piece[..., wide3:] for piece in attn_w])
    out_z = plan.over_z(out_t)
    outs = [out_t, out_z, plan.over_core(out_t), plan.over_core(out_z)]
    g0 = plan.swap_home(after(cotangent, x3))
    g1 = plan.over_z(g0)
    gs = [g0, g1, plan.over_core(g0), plan.over_core(g1)]

    attended, logs = call(
        attend_kernel,
        [((length, wide), BF), ((8, length), F32)],
        [ids, mixed],
        4 * length * length * wide,
    )
    att_z = plan.over_z(attended)
    att = [attended, att_z, plan.over_core(attended), plan.over_core(att_z)]

    hidden_own, normed_two, act, grad_up, gn2_first, gn2_second, up_bias_grad, down_t = call(
        lambda *refs: middle_kernel(n_w, shard, *refs),
        [
            ((rows, width), F32),
            ((length, width), BF),
            ((length, units), BF),
            ((length, units), BF),
            ((2, rows, width), F32),
            ((2, rows, width), BF),
            ((1, units), F32),
            ((width, units), BF),
        ],
        [ids]
        + att
        + outs
        + [x0, x1, x2, x3]
        + gs
        + [row(out_bias), row_gain_two, row_shift_two, up_bias_j]
        + mlp_w,
        2 * length * width * (width + 3 * units),
        [
            pltpu.VMEM((4, width, wide), BF),
            pltpu.VMEM((width, units), BF),
            pltpu.VMEM((width, 2 * units), BF),
        ],
    )
    gn2_core = plan.over_core(gn2_second)
    gn2_z = plan.over_z((gn2_first[1] + gn2_core[1].astype(F32)).astype(BF))
    mlp_grad = call(
        lambda *refs: mlp_grad_kernel(n_o, shard, *refs),
        grad_outs(2 * units),
        [ids, normed_two] + gs + [act, grad_up],
        4 * length * width * units,
        [pltpu.VMEM((width, 2 * units), F32)],
    )
    grad_hidden, gh0, sums_two = call(
        norm_two_kernel,
        [((rows, width), F32), ((rows, width), BF), ((8, width), F32)],
        [ids, gn2_first[0], gn2_core[0], gn2_z, hidden_own, g0, row_gain_two],
        20 * rows * width,
    )
    gh1 = plan.over_z(gh0)
    ghs = [gh0, gh1, plan.over_core(gh0), plan.over_core(gh1)]
    out_first, out_second = call(
        mlp_out_kernel,
        [((2, rows, width), F32), ((2, rows, width), BF)],
        [ids, act, down_t],
        2 * length * width * units,
    )
    mlp_own = plan.group_sum(out_first, out_second)
    output = plan.swap_home((hidden_own + mlp_own + down_bias).astype(BF))
    mlp_summed = plan.unspread(plane_total(mlp_grad).astype(BF).reshape(2, shard, 2 * units))

    grad_mixed, gn1_first, gn1_second, qkv_bias_grad, sums_one = call(
        attend_back_kernel,
        [
            ((length, wide3), BF),
            ((2, rows, width), F32),
            ((2, rows, width), BF),
            ((1, wide3), F32),
            ((8, width), F32),
        ],
        [ids, mixed, logs, w_all] + ghs + [x0, x1, x2, x3],
        10 * length * length * wide,
        [pltpu.VMEM((length, wide), F32), pltpu.VMEM((length, 3 * HEAD_DIM), F32)],
    )
    gn1_core = plan.over_core(gn1_second)
    gn1_z = plan.over_z((gn1_first[1] + gn1_core[1].astype(F32)).astype(BF))
    attn_grad = call(
        lambda *refs: attn_grad_kernel(n_o, shard, *refs),
        grad_outs(width),
        [ids, normed, grad_mixed] + ghs + [attended],
        2 * length * width * width,
        [pltpu.VMEM((width, width), F32)],
    )
    (grad_low,) = call(
        norm_one_kernel,
        [((rows, width), BF)],
        [ids, gn1_first[0], gn1_core[0], gn1_z, x0, row_gain_one, grad_hidden],
        20 * rows * width,
    )
    grad_tokens = plan.swap_home(grad_low).astype(F32)
    attn_summed = plan.unspread(plane_total(attn_grad).astype(BF).reshape(2, shard, width))

    qkv_bias_full = lax.dynamic_update_slice_in_dim(
        jnp.zeros((3, width), F32), qkv_bias_grad.reshape(3, wide), plan.j * wide, 1
    )
    up_bias_full = lax.dynamic_update_slice_in_dim(
        jnp.zeros((4 * units,), F32), up_bias_grad[0], plan.j * units, 0
    )
    small = jnp.concatenate(
        [
            sums_one[0],
            sums_one[1],
            sums_two[0],
            sums_two[1],
            sums_two[2],
            sums_two[3],
            qkv_bias_full.reshape(-1),
            up_bias_full,
        ]
    )
    small = plan.all_sum(small)
    vec = [small[i * width : (i + 1) * width] for i in range(6)]
    qkv_bias_summed = lax.dynamic_slice_in_dim(
        small[6 * width : 9 * width].reshape(3, width), plan.t * wide, wide, 1
    )
    up_bias_summed = lax.dynamic_slice_in_dim(small[9 * width :], plan.t * units, units, 0)
    return (
        output,
        grad_tokens,
        vec[0],
        vec[1],
        attn_summed[:, :wide3].reshape(shard, 3, wide),
        qkv_bias_summed,
        attn_summed[:, wide3:].T,
        vec[2],
        vec[3],
        vec[4],
        mlp_summed[:, :units],
        up_bias_summed,
        mlp_summed[:, units:].T,
        vec[5],
    )


def solution(mesh):
    in_specs = (
        P(("dp", "tensor"), None),
        P(),
        P(),
        P("dp", None, "tensor"),
        P(None, "tensor"),
        P("tensor", "dp"),
        P(),
        P(),
        P(),
        P("dp", "tensor"),
        P("tensor"),
        P("tensor", "dp"),
        P(),
        P(("dp", "tensor"), None),
    )
    out_specs = (
        P(("dp", "tensor"), None),
        P(("dp", "tensor"), None),
        P(),
        P(),
        P("dp", None, "tensor"),
        P(None, "tensor"),
        P("tensor", "dp"),
        P(),
        P(),
        P(),
        P("dp", "tensor"),
        P("tensor"),
        P("tensor", "dp"),
        P(),
    )
    return jax.shard_map(local, mesh=mesh, in_specs=in_specs, out_specs=out_specs, check_vma=False)
```

```python
import jax
import jax.numpy as jnp
from jax import lax
from jax.experimental import pallas as pl
from jax.experimental.pallas import tpu as pltpu
from jax.sharding import PartitionSpec as P

HEAD_DIM = 64
EPS = 1e-05
BF = jnp.bfloat16
F32 = jnp.float32
AXES = ("dp", "tensor")


def dot_nn(left, right):
    return lax.dot_general(left, right, (((1,), (0,)), ((), ())), preferred_element_type=F32)


def dot_nt(left, right):
    return lax.dot_general(left, right, (((1,), (1,)), ((), ())), preferred_element_type=F32)


def dot_tn(left, right):
    return lax.dot_general(left, right, (((0,), (0,)), ((), ())), preferred_element_type=F32)


class Plan:
    def __init__(self):
        self.n_dp = lax.axis_size("dp")
        self.n_t = lax.axis_size("tensor")
        assert self.n_t == 4 and self.n_dp % 2 == 0
        self.n_k = self.n_dp // 2
        assert self.n_k & (self.n_k - 1) == 0
        self.d = lax.axis_index("dp")
        self.t = lax.axis_index("tensor")
        self.k = self.d // 2
        self.c = self.d % 2
        self.h = self.t // 2
        self.r = jnp.where(self.c == self.h, self.t, self.t ^ 2)
        self.j = self.c + 2 * (self.t % 2)

    def send(self, value, where):
        pairs = []
        for d in range(self.n_dp):
            for t in range(self.n_t):
                to_d, to_t = where(d, t)
                pairs.append((d * self.n_t + t, to_d * self.n_t + to_t))
        return lax.ppermute(value, AXES, pairs)

    def swap_home(self, value):
        return self.send(value, lambda d, t: (d, t) if d % 2 == t // 2 else (d ^ 1, t ^ 2))

    def over_z(self, value):
        return self.send(value, lambda d, t: (d, t ^ 1))

    def over_core(self, value):
        return self.send(value, lambda d, t: (d ^ 1, t))

    def over_plane(self, value, p):
        return self.send(value, lambda d, t: (d ^ (2 * p), t))

    def group_gather(self, value):
        mine = jnp.stack([value, self.over_z(value)])
        return mine, self.over_core(mine)

    def group_sum(self, first, second):
        pair = first + self.over_core(second).astype(F32)
        return pair[0] + self.over_z(pair[1].astype(BF)).astype(F32)

    def spread(self, shard):
        got = []
        for i in (0, 1):
            got.append(
                self.send(
                    shard, lambda d, t, i=i: (2 * (d // 2) + t % 2, t // 2 + 2 * ((d % 2) ^ i))
                )
            )
        return got

    def to_slot(self, value):
        return self.send(value, lambda d, t: (2 * (d // 2) + t % 2, t // 2 + 2 * (d % 2)))

    def unspread(self, chunk):
        total = 0.0
        for i in (0, 1):
            part = lax.dynamic_index_in_dim(chunk, self.h ^ i, 0, keepdims=False)
            got = self.send(
                part, lambda d, t, i=i: (2 * (d // 2) + ((t // 2) ^ i), d % 2 + 2 * (t % 2))
            )
            total = total + got.astype(F32)
        return total

    def plane_gather(self, value):
        if self.n_k == 4:
            return jnp.stack([value] + [self.over_plane(value, p) for p in (1, 2, 3)])
        held = value[None]
        size = 1
        while size < self.n_k:
            held = jnp.concatenate([held, self.over_plane(held, size)])
            size *= 2
        return held

    def plane_sum(self, value):
        pick = lambda p: lax.dynamic_index_in_dim(value, self.k ^ p, 0, keepdims=False)
        if self.n_k == 4:
            total = pick(0).astype(F32)
            for p in (1, 2, 3):
                total = total + self.over_plane(pick(p).astype(BF), p).astype(F32)
            return total
        held = jnp.stack([pick(p) for p in range(self.n_k)]).astype(F32)
        size = self.n_k // 2
        while size:
            held = held[:size] + self.over_plane(held[size:].astype(BF), size).astype(F32)
            size //= 2
        return held[0]

    def ordered_weight(self, held):
        flat = held.reshape((self.n_dp,) + held.shape[2:])
        parts = []
        for d in range(self.n_dp):
            at = ((d // 2) ^ self.k) * 2 + ((d % 2) ^ self.h)
            parts.append(lax.dynamic_index_in_dim(flat, at, 0, keepdims=False))
        return jnp.concatenate(parts, 0)

    def ordered_rows(self, first, second):
        flat = jnp.concatenate([first, second])
        return jnp.concatenate(
            [lax.dynamic_index_in_dim(flat, a ^ self.r, 0, keepdims=False) for a in range(4)], 0
        )

    def relative_rows(self, value):
        rows = value.reshape((4, -1) + value.shape[1:])
        return [lax.dynamic_index_in_dim(rows, i ^ self.r, 0, keepdims=False) for i in range(4)]

    def chip_sum(self, value):
        value = value + self.over_core(value)
        p = 1
        while p < self.n_k:
            value = value + self.over_plane(value, p)
            p *= 2
        return value

    def over_two(self, value):
        return self.send(value, lambda d, t: (d, t ^ 2))


def after(value, *earlier):
    return lax.optimization_barrier((value,) + earlier)[0]


PEAK = 1.15e9


def call(body, outs, args, micros, mib, scratch=()):
    shapes = tuple(jax.ShapeDtypeStruct(shape, dtype) for shape, dtype in outs)
    cost = pl.CostEstimate(
        flops=int(micros * PEAK), bytes_accessed=int(micros * 3.0e6), transcendentals=0
    )

    return pl.pallas_call(
        body,
        out_shape=shapes,
        in_specs=[pl.BlockSpec(memory_space=pltpu.SMEM)]
        + [pl.BlockSpec(memory_space=pltpu.VMEM)] * (len(args) - 1),
        out_specs=tuple(pl.BlockSpec(memory_space=pltpu.VMEM) for _ in shapes),
        scratch_shapes=list(scratch),
        compiler_params=pltpu.CompilerParams(vmem_limit_bytes=mib * 2**20),
        cost_estimate=cost,
    )(*args)


def normalise(values):
    middle = jnp.mean(values, -1, keepdims=True)
    centred = values - middle
    variance = jnp.mean(centred * centred, -1, keepdims=True)
    rate = lax.rsqrt(variance + EPS)
    return centred * rate, rate


def norm_back(grad, hat, rate, gain):
    scaled = grad * gain
    first = jnp.mean(scaled, -1, keepdims=True)
    second = jnp.mean(scaled * hat, -1, keepdims=True)
    return rate * (scaled - first - hat * second)


def col_sum(values):
    return jnp.sum(values, 0, keepdims=True)


def chunk_at(ids, i, rows):
    return pl.ds(pl.multiple_of((ids[2] ^ i) * rows, rows), rows)


def order_weight(ids, pieces, scratch, shard):
    if len(pieces) == 1:
        scratch[...] = pieces[0][0]
        return
    for p, piece in enumerate(pieces):
        for i in range(2):
            at = 2 * (ids[0] ^ p) + (ids[1] ^ i)
            scratch[pl.ds(pl.multiple_of(at * shard, shard), shard), :] = piece[i]


def mixed_kernel(n_w, shard, ids, x0, x1, x2, x3, gain, shift, bias, *refs):
    pieces, (normed, mixed, w_all) = refs[:n_w], refs[n_w:]
    order_weight(ids, pieces, w_all, shard)
    wide = mixed.shape[1]
    for i, x in enumerate((x0, x1, x2, x3)):
        rows = x.shape[0]
        hat, _ = normalise(x[...].astype(F32))
        low = (hat * gain[...] + shift[...]).astype(BF)
        normed[chunk_at(ids, i, rows), :] = low
        out = dot_nn(low, w_all[:, :wide]) + bias[...]
        mixed[chunk_at(ids, i, rows), :] = out.astype(BF)


def attend_kernel(ids, mixed, attended, logs):
    length, wide = attended.shape
    block = min(256, length)
    tri = lax.broadcasted_iota(jnp.int32, (block, block), 0) <= lax.broadcasted_iota(
        jnp.int32, (block, block), 1
    )
    for head in range(wide // HEAD_DIM):
        at = head * HEAD_DIM
        q_t = (mixed[:, at : at + HEAD_DIM].astype(F32) * HEAD_DIM ** (-0.5)).T.astype(BF)
        keys = mixed[:, wide + at : wide + at + HEAD_DIM]
        v_t = mixed[:, 2 * wide + at : 2 * wide + at + HEAD_DIM].astype(F32).T.astype(BF)
        for b in range(length // block):
            low = b * block
            q_b = q_t[:, low : low + block]
            near = jnp.where(tri, dot_nn(keys[low : low + block], q_b), -1e30)
            top = jnp.max(near, 0, keepdims=True)
            if b:
                far = dot_nn(keys[:low], q_b)
                top = jnp.maximum(top, jnp.max(far, 0, keepdims=True))
            near = jnp.exp(near - top)
            total = col_sum(near)
            out = dot_nn(v_t[:, low : low + block], near.astype(BF))
            if b:
                far = jnp.exp(far - top)
                total = total + col_sum(far)
                out = out + dot_nn(v_t[:, :low], far.astype(BF))
            out = out * (1.0 / total)
            attended[low : low + block, at : at + HEAD_DIM] = out.T.astype(BF)
            logs[head : head + 1, low : low + block] = top + jnp.log(total)


def forward_kernel(n_w, shard, ids, *refs):
    att, outs, xs = refs[0:4], refs[4:8], refs[8:12]
    out_bias, gain, shift, up_bias = refs[12:16]
    pieces = refs[16 : 16 + n_w]
    hidden_own, normed_two, act, slope, up_w = refs[16 + n_w : 21 + n_w]
    out_w = refs[21 + n_w]
    order_weight(ids, pieces, up_w, shard)
    for g, out in enumerate(outs):
        if n_w == 1:
            out_w[g] = out[0, 0]
        else:
            for p in range(n_w):
                for i in range(2):
                    at = 2 * (ids[0] ^ p) + (ids[1] ^ i)
                    out_w[g, pl.ds(pl.multiple_of(at * shard, shard), shard), :] = out[p, i]
    for i in range(4):
        rows = xs[0].shape[0]
        hidden = xs[i][...].astype(F32) + out_bias[...]
        for g in range(4):
            hidden = hidden + dot_nt(att[g][chunk_at(ids, i, rows), :], out_w[g])
        if i == 0:
            hidden_own[...] = hidden
        hat, _ = normalise(hidden)
        low = (hat * gain[...] + shift[...]).astype(BF)
        span = slice(i * rows, (i + 1) * rows)
        normed_two[span, :] = low
        up = dot_nn(low, up_w[...]) + up_bias[...]
        whole = 0.5 * (1.0 + lax.erf(up * 0.5**0.5))
        act[span, :] = (up * whole).astype(BF)
        bell = jnp.exp(-0.5 * up * up) * (2.0 * jnp.pi) ** (-0.5)
        slope[span, :] = (whole + up * bell).astype(BF)


def backward_kernel(n_w, shard, ids, *refs):
    pieces = refs[:n_w]
    g0, g1, g2, g3, slope, up_w = refs[n_w : n_w + 6]
    grad_up, own, after_one, second, bias_grad, down_t = refs[n_w + 6 :]
    rows = g0.shape[0]
    units = slope.shape[1]
    order_weight(ids, pieces, down_t, shard)
    bias_sum = jnp.zeros((1, units), F32)
    for i, g in enumerate((g0, g1, g2, g3)):
        span = slice(i * rows, (i + 1) * rows)
        grad = (dot_nn(g[...], down_t[...]) * slope[span, :].astype(F32)).astype(BF)
        grad_up[span, :] = grad
        bias_sum = bias_sum + col_sum(grad.astype(F32))
        put_part(i, dot_nt(grad, up_w[...]), own, after_one, second)
    bias_grad[...] = bias_sum


def put_part(i, value, own, after_one, second):
    if i == 0:
        own[...] = value
    elif i == 1:
        after_one[...] = value
    else:
        second[i - 2] = value.astype(BF)


def mlp_grad_kernel(n_o, shard, ids, normed_two, g0, g1, g2, g3, act, grad_up, *refs):
    outs, scratch = refs[:n_o], refs[n_o]
    units = act.shape[1]
    rows = g0.shape[0]
    scratch[:, :units] = dot_tn(normed_two[...], grad_up[...])
    total = 0.0
    for i, g in enumerate((g0, g1, g2, g3)):
        total = total + dot_tn(g[...], act[i * rows : (i + 1) * rows, :])
    scratch[:, units:] = total
    emit_grad(ids, scratch, outs, shard)


def emit_grad(ids, scratch, outs, shard):
    if len(outs) == 1:
        outs[0][...] = scratch[...]
        return
    for p, out in enumerate(outs):
        at = pl.ds(pl.multiple_of((ids[0] ^ p) * 2 * shard, 2 * shard), 2 * shard)
        out[...] = scratch[at, :].astype(out.dtype)


def mlp_out_kernel(ids, act, down_t, own, after_one, second):
    rows = own.shape[0]
    for i in range(4):
        out = dot_nt(act[i * rows : (i + 1) * rows, :], down_t[...])
        put_part(i, out, own, after_one, second)


def norm_two_kernel(ids, own, got_core, got_z, hidden, g, gain, grad_hidden, low, sums):
    grad = own[...] + got_core[0].astype(F32) + got_z[...].astype(F32)
    hat, rate = normalise(hidden[...])
    g32 = g[...].astype(F32)
    total = g32 + norm_back(grad, hat, rate, gain[...])
    grad_hidden[...] = total
    low[...] = total.astype(BF)
    sums[0:1, :] = col_sum(total)
    sums[1:2, :] = col_sum(grad * hat)
    sums[2:3, :] = col_sum(grad)
    sums[3:4, :] = col_sum(g32)


def norm_one_kernel(ids, own, got_core, got_z, x, gain, grad_hidden, out):
    grad = own[...] + got_core[0].astype(F32) + got_z[...].astype(F32)
    hat, rate = normalise(x[...].astype(F32))
    total = grad_hidden[...] + norm_back(grad, hat, rate, gain[...])
    out[...] = total.astype(BF)


def attend_back_kernel(ids, mixed, logs, w_all, gh0, gh1, gh2, gh3, x0, x1, x2, x3, *refs):
    sums_two, up_bias, grad_mixed, own, after_one, second, small, g_rows, gm32 = refs
    length, wide3 = mixed.shape
    wide = wide3 // 3
    rows = x0.shape[0]
    block = min(256, length)
    for i, gh in enumerate((gh0, gh1, gh2, gh3)):
        g_rows[chunk_at(ids, i, rows), :] = dot_nn(gh[...], w_all[:, wide3:])
    tri = lax.broadcasted_iota(jnp.int32, (block, block), 0) <= lax.broadcasted_iota(
        jnp.int32, (block, block), 1
    )
    for head in range(wide // HEAD_DIM):
        at = head * HEAD_DIM
        scaled = mixed[:, at : at + HEAD_DIM].astype(F32) * HEAD_DIM ** (-0.5)
        q_rows = scaled.astype(BF)
        q_t = scaled.T.astype(BF)
        keys = mixed[:, wide + at : wide + at + HEAD_DIM]
        k_t = keys.astype(F32).T.astype(BF)
        values = mixed[:, 2 * wide + at : 2 * wide + at + HEAD_DIM]
        grad32 = g_rows[:, at : at + HEAD_DIM]
        grad_rows = grad32.astype(BF)
        grad_t = grad32.T.astype(BF)
        for b in range(length // block):
            low, end = b * block, (b + 1) * block
            q_b = q_t[:, low:end]
            g_b = grad_t[:, low:end]
            log = logs[head : head + 1, low:end]
            near = jnp.where(tri, jnp.exp(dot_nn(keys[low:end], q_b) - log), 0.0)
            near_d = dot_nn(values[low:end], g_b)
            inner = col_sum(near * near_d)
            if b:
                far = jnp.exp(dot_nn(keys[:low], q_b) - log)
                far_d = dot_nn(values[:low], g_b)
                inner = inner + col_sum(far * far_d)
            near_s = (near * (near_d - inner)).astype(BF)
            grad_q = dot_nn(k_t[:, low:end], near_s)
            gm32[low:end, HEAD_DIM : 2 * HEAD_DIM] = dot_nn(near_s, q_rows[low:end])
            gm32[low:end, 2 * HEAD_DIM :] = dot_nn(near.astype(BF), grad_rows[low:end])
            if b:
                far_s = (far * (far_d - inner)).astype(BF)
                grad_q = grad_q + dot_nn(k_t[:, :low], far_s)
                gm32[:low, HEAD_DIM : 2 * HEAD_DIM] += dot_nn(far_s, q_rows[low:end])
                gm32[:low, 2 * HEAD_DIM :] += dot_nn(far.astype(BF), grad_rows[low:end])
            gm32[low:end, :HEAD_DIM] = grad_q.T * HEAD_DIM ** (-0.5)
        for part in range(3):
            grad_mixed[:, part * wide + at : part * wide + at + HEAD_DIM] = gm32[
                :, part * HEAD_DIM : (part + 1) * HEAD_DIM
            ].astype(BF)
    bias_grad = col_sum(grad_mixed[...].astype(F32))
    gain_sum = jnp.zeros((1, x0.shape[1]), F32)
    shift_sum = gain_sum
    for i, x in enumerate((x0, x1, x2, x3)):
        back = dot_nt(grad_mixed[chunk_at(ids, i, rows), :], w_all[:, :wide3])
        hat, _ = normalise(x[...].astype(F32))
        gain_sum = gain_sum + col_sum(back * hat)
        shift_sum = shift_sum + col_sum(back)
        put_part(i, back, own, after_one, second)
    small[...] = jnp.zeros(small.shape, F32)
    small[0:1, :] = gain_sum
    small[1:2, :] = shift_sum
    small[2:6, :] = sums_two[0:4, :]
    small[pl.ds(6 + 2 * ids[3], 1), :wide3] = bias_grad
    small[pl.ds(7 + 2 * ids[3], 1), : up_bias.shape[1]] = up_bias[...]


def attn_grad_kernel(n_o, shard, ids, normed, grad_mixed, gh0, gh1, gh2, gh3, attended, *refs):
    outs, scratch = refs[:n_o], refs[n_o]
    wide3 = grad_mixed.shape[1]
    rows = gh0.shape[0]
    scratch[:, :wide3] = dot_tn(normed[...], grad_mixed[...])
    total = 0.0
    for i, gh in enumerate((gh0, gh1, gh2, gh3)):
        total = total + dot_tn(gh[...], attended[chunk_at(ids, i, rows), :])
    scratch[:, wide3:] = total
    emit_grad(ids, scratch, outs, shard)


def local(
    tokens,
    gain_one,
    shift_one,
    qkv_weight,
    qkv_bias,
    out_weight,
    out_bias,
    gain_two,
    shift_two,
    up_weight,
    up_bias,
    down_weight,
    down_bias,
    cotangent,
):
    plan = Plan()
    rows, width = tokens.shape
    shard = qkv_weight.shape[0]
    wide = qkv_weight.shape[2]
    wide3 = 3 * wide
    units = up_weight.shape[1]
    length = 4 * rows
    n_k = plan.n_k
    direct = n_k == 4 and shard % 16 == 0
    n_w = n_k if direct else 1
    n_o = n_k if direct else 1
    ids = jnp.stack([plan.k, plan.h, plan.r, plan.j]).astype(jnp.int32)
    row = lambda v: v.reshape(1, -1)
    row_gain_one, row_shift_one = row(gain_one), row(shift_one)
    row_gain_two, row_shift_two = row(gain_two), row(shift_two)

    def plane_pieces(value):
        if direct:
            return [value] + [plan.over_plane(value, p) for p in (1, 2, 3)]
        return [plan.ordered_weight(plan.plane_gather(value))[None]]

    def plane_got(pieces):
        return [plan.over_plane(pieces[p], p) for p in (1, 2, 3)] if direct else []

    def plane_total(pieces, got, *earlier):
        if direct:
            total = after(pieces[0], *earlier)
            for value in got:
                total = total + value.astype(F32)
            return total
        return plan.plane_sum(pieces[0].reshape((n_k, 2 * shard) + pieces[0].shape[1:]))

    def grad_outs(n):
        if direct:
            return [((2 * shard, n), F32)] + [((2 * shard, n), BF)] * (n_k - 1)
        return [((width, n), F32)]

    def parts():
        return [((rows, width), F32), ((rows, width), F32), ((2, rows, width), BF)]

    def toward_z(after_one, got_core):
        return (after_one + got_core[1].astype(F32)).astype(BF)

    x0 = plan.swap_home(tokens)
    attn_shard = jnp.concatenate([qkv_weight.reshape(shard, wide3), out_weight.T], 1)
    attn_spread = jnp.stack(plan.spread(attn_shard))
    biases = plan.to_slot(jnp.concatenate([qkv_bias.reshape(-1), up_bias]))
    qkv_bias_j, up_bias_j = row(biases[:wide3]), row(biases[wide3:])
    x1 = plan.over_z(x0)
    x2 = plan.over_core(x0)
    x3 = plan.over_core(x1)
    attn_w = plane_pieces(attn_spread)

    mlp_shard = jnp.concatenate([up_weight, down_weight.T], 1)
    mlp_spread = plan.spread(after(mlp_shard, attn_w[-1], x0))
    up_stack = jnp.stack([piece[:, :units] for piece in mlp_spread])
    down_stack = jnp.stack([piece[:, units:] for piece in mlp_spread])

    normed, mixed, w_all = call(
        lambda *refs: mixed_kernel(n_w, shard, *refs),
        [((length, width), BF), ((length, wide3), BF), ((width, width), BF)],
        [ids, x0, x1, x2, x3, row_gain_one, row_shift_one, qkv_bias_j] + attn_w,
        3,
        11,
    )
    out_t = jnp.stack([piece[..., wide3:] for piece in attn_w])
    out_z = plan.over_z(after(out_t, mixed))
    outs = [out_t, out_z, plan.over_core(out_t), plan.over_core(out_z)]
    g0 = plan.swap_home(after(cotangent, x1))
    up_pieces = plane_pieces(up_stack)

    attended, logs = call(
        attend_kernel,
        [((length, wide), BF), ((8, length), F32)],
        [ids, mixed],
        6,
        10,
    )
    att_z = plan.over_z(after(attended, g0, *up_pieces))
    down_pieces = plane_pieces(after(down_stack, attended))
    att_last = after(att_z, *outs, *down_pieces[1:])
    att = [attended, att_z, plan.over_core(attended), plan.over_core(att_last)]
    g1 = plan.over_z(after(g0, att_z))

    hidden_own, normed_two, act, slope, up_j = call(
        lambda *refs: forward_kernel(n_w, shard, *refs),
        [
            ((rows, width), F32),
            ((length, width), BF),
            ((length, units), BF),
            ((length, units), BF),
            ((width, units), BF),
        ],
        [ids]
        + att
        + outs
        + [x0, x1, x2, x3]
        + [row(out_bias), row_gain_two, row_shift_two, up_bias_j]
        + up_pieces,
        7,
        22,
        [pltpu.VMEM((4, width, wide), BF)],
    )
    gs = [g0, g1, plan.over_core(g0), plan.over_core(after(g1, slope))]
    grad_up, gn2_own, gn2_one, gn2_second, up_bias_grad, down_t = call(
        lambda *refs: backward_kernel(n_w, shard, *refs),
        [((length, units), BF)] + parts() + [((1, units), F32), ((width, units), BF)],
        [ids] + down_pieces + gs + [slope, up_j],
        5,
        18,
    )
    gn2_core = plan.over_core(gn2_second)
    gn2_z_in = toward_z(gn2_one, gn2_core)
    gn2_z = plan.over_z(gn2_z_in)
    out_own, out_one, out_second = call(
        mlp_out_kernel,
        parts(),
        [ids, act, down_t],
        2,
        12,
    )
    out_core = plan.over_core(out_second)
    out_z_in = toward_z(out_one, out_core)
    mlp_grad = call(
        lambda *refs: mlp_grad_kernel(n_o, shard, *refs),
        grad_outs(2 * units),
        [ids, after(normed_two, gn2_z_in)] + gs + [act, grad_up],
        5,
        22,
        [pltpu.VMEM((width, 2 * units), F32)],
    )
    grad_hidden, gh0, sums_two = call(
        norm_two_kernel,
        [((rows, width), F32), ((rows, width), BF), ((8, width), F32)],
        [ids, gn2_own, gn2_core, gn2_z, after(hidden_own, mlp_grad[-1]), g0, row_gain_two],
        2,
        8,
    )
    gh1 = plan.over_z(gh0)
    mlp_got = plane_got(mlp_grad)
    ghs = [gh0, gh1, plan.over_core(gh0), plan.over_core(after(gh1, *mlp_got[:2]))]
    out_from_z = plan.over_z(after(out_z_in, gh1))
    out_sum = hidden_own + out_own + out_core[0].astype(F32) + out_from_z.astype(F32)
    output_here = (out_sum + down_bias).astype(BF)

    grad_mixed, gn1_own, gn1_one, gn1_second, small = call(
        attend_back_kernel,
        [((length, wide3), BF)] + parts() + [((16, width), F32)],
        [ids, after(mixed, out_z_in), logs, w_all]
        + ghs
        + [x0, x1, x2, x3, sums_two, up_bias_grad],
        12,
        22,
        [pltpu.VMEM((length, wide), F32), pltpu.VMEM((length, 3 * HEAD_DIM), F32)],
    )
    gn1_core = plan.over_core(after(gn1_second, out_from_z, *mlp_got[2:]))
    gn1_z_in = toward_z(gn1_one, gn1_core)
    gn1_z = plan.over_z(gn1_z_in)
    mlp_part = plane_total(mlp_grad, mlp_got, gn1_z_in).astype(BF).reshape(2, shard, 2 * units)
    mlp_summed = plan.unspread(mlp_part)
    attn_grad = call(
        lambda *refs: attn_grad_kernel(n_o, shard, *refs),
        grad_outs(width),
        [ids, after(normed, gn1_z_in), grad_mixed] + ghs + [attended],
        3,
        14,
        [pltpu.VMEM((width, width), F32)],
    )
    small = plan.chip_sum(after(small, gn1_z_in))
    attn_grad = lax.optimization_barrier(tuple(attn_grad) + (mlp_summed, small))[:-2]
    attn_got = plane_got(attn_grad)
    (grad_low,) = call(
        norm_one_kernel,
        [((rows, width), BF)],
        [ids, gn1_own, gn1_core, gn1_z, x0, row_gain_one, grad_hidden],
        2,
        12,
    )
    grad_tokens = plan.swap_home(grad_low).astype(F32)
    output = plan.swap_home(after(output_here, gn1_z_in))

    small = after(small, grad_low)
    small = small + plan.over_z(small)
    attn_total = plane_total(attn_grad, attn_got, small, output)
    attn_part = attn_total.astype(BF).reshape(2, shard, width)
    attn_summed = plan.unspread(after(attn_part, grad_tokens))
    small = small + plan.over_two(small)
    mine = lax.dynamic_slice_in_dim(small, 6 + 2 * plan.t, 2, 0)
    return (
        output,
        grad_tokens,
        small[0],
        small[1],
        attn_summed[:, :wide3].reshape(shard, 3, wide),
        mine[0, :wide3].reshape(3, wide),
        attn_summed[:, wide3:].T,
        small[2],
        small[3],
        small[4],
        mlp_summed[:, :units],
        mine[1, :units],
        mlp_summed[:, units:].T,
        small[5],
    )


def solution(mesh):
    in_specs = (
        P(("dp", "tensor"), None),
        P(),
        P(),
        P("dp", None, "tensor"),
        P(None, "tensor"),
        P("tensor", "dp"),
        P(),
        P(),
        P(),
        P("dp", "tensor"),
        P("tensor"),
        P("tensor", "dp"),
        P(),
        P(("dp", "tensor"), None),
    )
    out_specs = (
        P(("dp", "tensor"), None),
        P(("dp", "tensor"), None),
        P(),
        P(),
        P("dp", None, "tensor"),
        P(None, "tensor"),
        P("tensor", "dp"),
        P(),
        P(),
        P(),
        P("dp", "tensor"),
        P("tensor"),
        P("tensor", "dp"),
        P(),
    )
    return jax.shard_map(local, mesh=mesh, in_specs=in_specs, out_specs=out_specs, check_vma=False)
```

```python
import jax
import jax.numpy as jnp
from jax import lax
from jax.experimental import pallas as pl
from jax.experimental.pallas import tpu as pltpu
from jax.sharding import PartitionSpec as P

HEAD_DIM = 64
EPS = 1e-05
BF = jnp.bfloat16
F32 = jnp.float32
AXES = ("dp", "tensor")


def dot_nn(left, right):
    return lax.dot_general(left, right, (((1,), (0,)), ((), ())), preferred_element_type=F32)


def dot_nt(left, right):
    return lax.dot_general(left, right, (((1,), (1,)), ((), ())), preferred_element_type=F32)


def dot_tn(left, right):
    return lax.dot_general(left, right, (((0,), (0,)), ((), ())), preferred_element_type=F32)


class Plan:
    def __init__(self):
        self.n_dp = lax.axis_size("dp")
        self.n_t = lax.axis_size("tensor")
        assert self.n_t == 4 and self.n_dp % 2 == 0
        self.n_k = self.n_dp // 2
        assert self.n_k & (self.n_k - 1) == 0
        self.d = lax.axis_index("dp")
        self.t = lax.axis_index("tensor")
        self.k = self.d // 2
        self.c = self.d % 2
        self.h = self.t // 2
        self.r = jnp.where(self.c == self.h, self.t, self.t ^ 2)
        self.j = self.c + 2 * (self.t % 2)

    def send(self, value, where):
        pairs = []
        for d in range(self.n_dp):
            for t in range(self.n_t):
                to_d, to_t = where(d, t)
                pairs.append((d * self.n_t + t, to_d * self.n_t + to_t))
        return lax.ppermute(value, AXES, pairs)

    def swap_home(self, value):
        return self.send(value, lambda d, t: (d, t) if d % 2 == t // 2 else (d ^ 1, t ^ 2))

    def swap_next(self, value):
        return self.send(value, lambda d, t: (d, t ^ 1) if d % 2 == t // 2 else (d ^ 1, t ^ 3))

    def over_z(self, value):
        return self.send(value, lambda d, t: (d, t ^ 1))

    def over_core(self, value):
        return self.send(value, lambda d, t: (d ^ 1, t))

    def over_plane(self, value, p):
        return self.send(value, lambda d, t: (d ^ (2 * p), t))

    def group_gather(self, value):
        mine = jnp.stack([value, self.over_z(value)])
        return mine, self.over_core(mine)

    def group_sum(self, first, second):
        pair = first + self.over_core(second).astype(F32)
        return pair[0] + self.over_z(pair[1].astype(BF)).astype(F32)

    def spread(self, shard):
        got = []
        for i in (0, 1):
            got.append(
                self.send(
                    shard, lambda d, t, i=i: (2 * (d // 2) + t % 2, t // 2 + 2 * ((d % 2) ^ i))
                )
            )
        return got

    def to_slot(self, value):
        return self.send(value, lambda d, t: (2 * (d // 2) + t % 2, t // 2 + 2 * (d % 2)))

    def unspread(self, chunk):
        total = 0.0
        for i in (0, 1):
            part = lax.dynamic_index_in_dim(chunk, self.h ^ i, 0, keepdims=False)
            got = self.send(
                part, lambda d, t, i=i: (2 * (d // 2) + ((t // 2) ^ i), d % 2 + 2 * (t % 2))
            )
            total = total + got.astype(F32)
        return total

    def plane_gather(self, value):
        if self.n_k == 4:
            return jnp.stack([value] + [self.over_plane(value, p) for p in (1, 2, 3)])
        held = value[None]
        size = 1
        while size < self.n_k:
            held = jnp.concatenate([held, self.over_plane(held, size)])
            size *= 2
        return held

    def plane_sum(self, value):
        pick = lambda p: lax.dynamic_index_in_dim(value, self.k ^ p, 0, keepdims=False)
        if self.n_k == 4:
            total = pick(0).astype(F32)
            for p in (1, 2, 3):
                total = total + self.over_plane(pick(p).astype(BF), p).astype(F32)
            return total
        held = jnp.stack([pick(p) for p in range(self.n_k)]).astype(F32)
        size = self.n_k // 2
        while size:
            held = held[:size] + self.over_plane(held[size:].astype(BF), size).astype(F32)
            size //= 2
        return held[0]

    def ordered_weight(self, held):
        flat = held.reshape((self.n_dp,) + held.shape[2:])
        parts = []
        for d in range(self.n_dp):
            at = ((d // 2) ^ self.k) * 2 + ((d % 2) ^ self.h)
            parts.append(lax.dynamic_index_in_dim(flat, at, 0, keepdims=False))
        return jnp.concatenate(parts, 0)

    def ordered_rows(self, first, second):
        flat = jnp.concatenate([first, second])
        return jnp.concatenate(
            [lax.dynamic_index_in_dim(flat, a ^ self.r, 0, keepdims=False) for a in range(4)], 0
        )

    def relative_rows(self, value):
        rows = value.reshape((4, -1) + value.shape[1:])
        return [lax.dynamic_index_in_dim(rows, i ^ self.r, 0, keepdims=False) for i in range(4)]

    def chip_sum(self, value):
        value = value + self.over_core(value)
        p = 1
        while p < self.n_k:
            value = value + self.over_plane(value, p)
            p *= 2
        return value

    def over_two(self, value):
        return self.send(value, lambda d, t: (d, t ^ 2))


def after(value, *earlier):
    return lax.optimization_barrier((value,) + earlier)[0]


PEAK = 1.15e9


def call(body, outs, args, micros, mib, scratch=()):
    shapes = tuple(jax.ShapeDtypeStruct(shape, dtype) for shape, dtype in outs)
    cost = pl.CostEstimate(
        flops=int(micros * PEAK), bytes_accessed=int(micros * 3.0e6), transcendentals=0
    )

    return pl.pallas_call(
        body,
        out_shape=shapes,
        in_specs=[pl.BlockSpec(memory_space=pltpu.SMEM)]
        + [pl.BlockSpec(memory_space=pltpu.VMEM)] * (len(args) - 1),
        out_specs=tuple(pl.BlockSpec(memory_space=pltpu.VMEM) for _ in shapes),
        scratch_shapes=list(scratch),
        compiler_params=pltpu.CompilerParams(vmem_limit_bytes=mib * 2**20),
        cost_estimate=cost,
    )(*args)


def normalise(values):
    middle = jnp.mean(values, -1, keepdims=True)
    centred = values - middle
    variance = jnp.mean(centred * centred, -1, keepdims=True)
    rate = lax.rsqrt(variance + EPS)
    return centred * rate, rate


def norm_back(grad, hat, rate, gain):
    scaled = grad * gain
    first = jnp.mean(scaled, -1, keepdims=True)
    second = jnp.mean(scaled * hat, -1, keepdims=True)
    return rate * (scaled - first - hat * second)


def col_sum(values):
    return jnp.sum(values, 0, keepdims=True)


def chunk_at(ids, i, rows):
    return pl.ds(pl.multiple_of((ids[2] ^ i) * rows, rows), rows)


def order_weight(ids, pieces, scratch, shard):
    if len(pieces) == 1:
        scratch[...] = pieces[0][0]
        return
    for p, piece in enumerate(pieces):
        for i in range(2):
            at = 2 * (ids[0] ^ p) + (ids[1] ^ i)
            scratch[pl.ds(pl.multiple_of(at * shard, shard), shard), :] = piece[i]


def mixed_kernel(n_w, shard, ids, x0, x1, x2, x3, gain, shift, bias, *refs):
    pieces, (normed, mixed, w_all) = refs[:n_w], refs[n_w:]
    order_weight(ids, pieces, w_all, shard)
    wide = mixed.shape[1]
    for i, x in enumerate((x0, x1, x2, x3)):
        rows = x.shape[0]
        hat, _ = normalise(x[...].astype(F32))
        low = (hat * gain[...] + shift[...]).astype(BF)
        normed[chunk_at(ids, i, rows), :] = low
        out = dot_nn(low, w_all[:, :wide]) + bias[...]
        mixed[chunk_at(ids, i, rows), :] = out.astype(BF)


def attend_kernel(ids, mixed, attended, logs):
    length, wide = attended.shape
    block = min(256, length)
    tri = lax.broadcasted_iota(jnp.int32, (block, block), 0) <= lax.broadcasted_iota(
        jnp.int32, (block, block), 1
    )
    for head in range(wide // HEAD_DIM):
        at = head * HEAD_DIM
        q_t = (mixed[:, at : at + HEAD_DIM].astype(F32) * HEAD_DIM ** (-0.5)).T.astype(BF)
        keys = mixed[:, wide + at : wide + at + HEAD_DIM]
        v_t = mixed[:, 2 * wide + at : 2 * wide + at + HEAD_DIM].astype(F32).T.astype(BF)
        for b in range(length // block):
            low = b * block
            q_b = q_t[:, low : low + block]
            near = jnp.where(tri, dot_nn(keys[low : low + block], q_b), -1e30)
            top = jnp.max(near, 0, keepdims=True)
            if b:
                far = dot_nn(keys[:low], q_b)
                top = jnp.maximum(top, jnp.max(far, 0, keepdims=True))
            near = jnp.exp(near - top)
            total = col_sum(near)
            out = dot_nn(v_t[:, low : low + block], near.astype(BF))
            if b:
                far = jnp.exp(far - top)
                total = total + col_sum(far)
                out = out + dot_nn(v_t[:, :low], far.astype(BF))
            out = out * (1.0 / total)
            attended[low : low + block, at : at + HEAD_DIM] = out.T.astype(BF)
            logs[head : head + 1, low : low + block] = top + jnp.log(total)


def forward_kernel(n_w, shard, ids, *refs):
    att, outs, xs = refs[0:4], refs[4:8], refs[8:12]
    out_bias, gain, shift, up_bias = refs[12:16]
    pieces = refs[16 : 16 + n_w]
    hidden_own, normed_two, act, slope, up_w = refs[16 + n_w : 21 + n_w]
    out_w = refs[21 + n_w]
    order_weight(ids, pieces, up_w, shard)
    for g, out in enumerate(outs):
        if n_w == 1:
            out_w[g] = out[0, 0]
        else:
            for p in range(n_w):
                for i in range(2):
                    at = 2 * (ids[0] ^ p) + (ids[1] ^ i)
                    out_w[g, pl.ds(pl.multiple_of(at * shard, shard), shard), :] = out[p, i]
    for i in range(4):
        rows = xs[0].shape[0]
        hidden = xs[i][...].astype(F32) + out_bias[...]
        for g in range(4):
            hidden = hidden + dot_nt(att[g][chunk_at(ids, i, rows), :], out_w[g])
        if i == 0:
            hidden_own[...] = hidden
        hat, _ = normalise(hidden)
        low = (hat * gain[...] + shift[...]).astype(BF)
        span = slice(i * rows, (i + 1) * rows)
        normed_two[span, :] = low
        up = dot_nn(low, up_w[...]) + up_bias[...]
        whole = 0.5 * (1.0 + lax.erf(up * 0.5**0.5))
        act[span, :] = (up * whole).astype(BF)
        bell = jnp.exp(-0.5 * up * up) * (2.0 * jnp.pi) ** (-0.5)
        slope[span, :] = (whole + up * bell).astype(BF)


def backward_kernel(n_w, shard, ids, *refs):
    pieces = refs[:n_w]
    g0, g1, g2, g3, slope, up_w = refs[n_w : n_w + 6]
    grad_up, own, after_one, second, bias_grad, down_t = refs[n_w + 6 :]
    rows = g0.shape[0]
    units = slope.shape[1]
    order_weight(ids, pieces, down_t, shard)
    bias_sum = jnp.zeros((1, units), F32)
    for i, g in enumerate((g0, g1, g2, g3)):
        span = slice(i * rows, (i + 1) * rows)
        grad = (dot_nn(g[...], down_t[...]) * slope[span, :].astype(F32)).astype(BF)
        grad_up[span, :] = grad
        bias_sum = bias_sum + col_sum(grad.astype(F32))
        put_part(i, dot_nt(grad, up_w[...]), own, after_one, second)
    bias_grad[...] = bias_sum


def put_part(i, value, own, after_one, second):
    if i == 0:
        own[...] = value
    elif i == 1:
        after_one[...] = value
    else:
        second[i - 2] = value.astype(BF)


def mlp_grad_kernel(n_o, shard, ids, normed_two, g0, g1, g2, g3, act, grad_up, *refs):
    outs, scratch = refs[:n_o], refs[n_o]
    units = act.shape[1]
    rows = g0.shape[0]
    scratch[:, :units] = dot_tn(normed_two[...], grad_up[...])
    total = 0.0
    for i, g in enumerate((g0, g1, g2, g3)):
        total = total + dot_tn(g[...], act[i * rows : (i + 1) * rows, :])
    scratch[:, units:] = total
    emit_grad(ids, scratch, outs, shard)


def emit_grad(ids, scratch, outs, shard):
    if len(outs) == 1:
        outs[0][...] = scratch[...]
        return
    for p, out in enumerate(outs):
        at = pl.ds(pl.multiple_of((ids[0] ^ p) * 2 * shard, 2 * shard), 2 * shard)
        out[...] = scratch[at, :].astype(out.dtype)


def mlp_out_kernel(ids, act, down_t, own, after_one, second):
    rows = own.shape[0]
    for i in range(4):
        out = dot_nt(act[i * rows : (i + 1) * rows, :], down_t[...])
        put_part(i, out, own, after_one, second)


def norm_two_kernel(ids, own, got_core, got_z, hidden, g, gain, grad_hidden, low, sums):
    grad = own[...] + got_core[0].astype(F32) + got_z[...].astype(F32)
    hat, rate = normalise(hidden[...])
    g32 = g[...].astype(F32)
    total = g32 + norm_back(grad, hat, rate, gain[...])
    grad_hidden[...] = total
    low[...] = total.astype(BF)
    sums[0:1, :] = col_sum(total)
    sums[1:2, :] = col_sum(grad * hat)
    sums[2:3, :] = col_sum(grad)
    sums[3:4, :] = col_sum(g32)


def norm_one_kernel(ids, own, got_core, got_z, x, gain, grad_hidden, out):
    grad = own[...] + got_core[0].astype(F32) + got_z[...].astype(F32)
    hat, rate = normalise(x[...].astype(F32))
    total = grad_hidden[...] + norm_back(grad, hat, rate, gain[...])
    out[...] = total.astype(BF)


def attend_back_kernel(ids, mixed, logs, w_all, gh0, gh1, gh2, gh3, x0, x1, x2, x3, *refs):
    sums_two, up_bias, grad_mixed, own, after_one, second, small, g_rows, gm32 = refs
    length, wide3 = mixed.shape
    wide = wide3 // 3
    rows = x0.shape[0]
    block = min(256, length)
    for i, gh in enumerate((gh0, gh1, gh2, gh3)):
        g_rows[chunk_at(ids, i, rows), :] = dot_nn(gh[...], w_all[:, wide3:])
    tri = lax.broadcasted_iota(jnp.int32, (block, block), 0) <= lax.broadcasted_iota(
        jnp.int32, (block, block), 1
    )
    for head in range(wide // HEAD_DIM):
        at = head * HEAD_DIM
        scaled = mixed[:, at : at + HEAD_DIM].astype(F32) * HEAD_DIM ** (-0.5)
        q_rows = scaled.astype(BF)
        q_t = scaled.T.astype(BF)
        keys = mixed[:, wide + at : wide + at + HEAD_DIM]
        k_t = keys.astype(F32).T.astype(BF)
        values = mixed[:, 2 * wide + at : 2 * wide + at + HEAD_DIM]
        grad32 = g_rows[:, at : at + HEAD_DIM]
        grad_rows = grad32.astype(BF)
        grad_t = grad32.T.astype(BF)
        for b in range(length // block):
            low, end = b * block, (b + 1) * block
            q_b = q_t[:, low:end]
            g_b = grad_t[:, low:end]
            log = logs[head : head + 1, low:end]
            near = jnp.where(tri, jnp.exp(dot_nn(keys[low:end], q_b) - log), 0.0)
            near_d = dot_nn(values[low:end], g_b)
            inner = col_sum(near * near_d)
            if b:
                far = jnp.exp(dot_nn(keys[:low], q_b) - log)
                far_d = dot_nn(values[:low], g_b)
                inner = inner + col_sum(far * far_d)
            near_s = (near * (near_d - inner)).astype(BF)
            grad_q = dot_nn(k_t[:, low:end], near_s)
            gm32[low:end, HEAD_DIM : 2 * HEAD_DIM] = dot_nn(near_s, q_rows[low:end])
            gm32[low:end, 2 * HEAD_DIM :] = dot_nn(near.astype(BF), grad_rows[low:end])
            if b:
                far_s = (far * (far_d - inner)).astype(BF)
                grad_q = grad_q + dot_nn(k_t[:, :low], far_s)
                gm32[:low, HEAD_DIM : 2 * HEAD_DIM] += dot_nn(far_s, q_rows[low:end])
                gm32[:low, 2 * HEAD_DIM :] += dot_nn(far.astype(BF), grad_rows[low:end])
            gm32[low:end, :HEAD_DIM] = grad_q.T * HEAD_DIM ** (-0.5)
        for part in range(3):
            grad_mixed[:, part * wide + at : part * wide + at + HEAD_DIM] = gm32[
                :, part * HEAD_DIM : (part + 1) * HEAD_DIM
            ].astype(BF)
    bias_grad = col_sum(grad_mixed[...].astype(F32))
    gain_sum = jnp.zeros((1, x0.shape[1]), F32)
    shift_sum = gain_sum
    for i, x in enumerate((x0, x1, x2, x3)):
        back = dot_nt(grad_mixed[chunk_at(ids, i, rows), :], w_all[:, :wide3])
        hat, _ = normalise(x[...].astype(F32))
        gain_sum = gain_sum + col_sum(back * hat)
        shift_sum = shift_sum + col_sum(back)
        put_part(i, back, own, after_one, second)
    small[...] = jnp.zeros(small.shape, F32)
    small[0:1, :] = gain_sum
    small[1:2, :] = shift_sum
    small[2:6, :] = sums_two[0:4, :]
    small[pl.ds(6 + 2 * ids[3], 1), :wide3] = bias_grad
    small[pl.ds(7 + 2 * ids[3], 1), : up_bias.shape[1]] = up_bias[...]


def attn_grad_kernel(n_o, shard, ids, normed, grad_mixed, gh0, gh1, gh2, gh3, attended, *refs):
    outs, scratch = refs[:n_o], refs[n_o]
    wide3 = grad_mixed.shape[1]
    rows = gh0.shape[0]
    scratch[:, :wide3] = dot_tn(normed[...], grad_mixed[...])
    total = 0.0
    for i, gh in enumerate((gh0, gh1, gh2, gh3)):
        total = total + dot_tn(gh[...], attended[chunk_at(ids, i, rows), :])
    scratch[:, wide3:] = total
    emit_grad(ids, scratch, outs, shard)


def local(
    tokens,
    gain_one,
    shift_one,
    qkv_weight,
    qkv_bias,
    out_weight,
    out_bias,
    gain_two,
    shift_two,
    up_weight,
    up_bias,
    down_weight,
    down_bias,
    cotangent,
):
    plan = Plan()
    rows, width = tokens.shape
    shard = qkv_weight.shape[0]
    wide = qkv_weight.shape[2]
    wide3 = 3 * wide
    units = up_weight.shape[1]
    length = 4 * rows
    n_k = plan.n_k
    direct = n_k == 4 and shard % 16 == 0
    n_w = n_k if direct else 1
    n_o = n_k if direct else 1
    ids = jnp.stack([plan.k, plan.h, plan.r, plan.j]).astype(jnp.int32)
    row = lambda v: v.reshape(1, -1)
    row_gain_one, row_shift_one = row(gain_one), row(shift_one)
    row_gain_two, row_shift_two = row(gain_two), row(shift_two)

    def plane_pieces(value):
        if direct:
            return [value] + [plan.over_plane(value, p) for p in (1, 2, 3)]
        return [plan.ordered_weight(plan.plane_gather(value))[None]]

    def plane_got(pieces):
        return [plan.over_plane(pieces[p], p) for p in (1, 2, 3)] if direct else []

    def plane_total(pieces, got, *earlier):
        if direct:
            total = after(pieces[0], *earlier)
            for value in got:
                total = total + value.astype(F32)
            return total
        return plan.plane_sum(pieces[0].reshape((n_k, 2 * shard) + pieces[0].shape[1:]))

    def grad_outs(n):
        if direct:
            return [((2 * shard, n), F32)] + [((2 * shard, n), BF)] * (n_k - 1)
        return [((width, n), F32)]

    def parts():
        return [((rows, width), F32), ((rows, width), F32), ((2, rows, width), BF)]

    def toward_z(after_one, got_core):
        return (after_one + got_core[1].astype(F32)).astype(BF)

    x0 = plan.swap_home(tokens)
    attn_shard = jnp.concatenate([qkv_weight.reshape(shard, wide3), out_weight.T], 1)
    attn_spread = jnp.stack(plan.spread(attn_shard))
    biases = plan.to_slot(jnp.concatenate([qkv_bias.reshape(-1), up_bias]))
    qkv_bias_j, up_bias_j = row(biases[:wide3]), row(biases[wide3:])
    x1 = plan.over_z(x0)
    x2 = plan.over_core(x0)
    x3 = plan.over_core(x1)
    attn_w = plane_pieces(attn_spread)

    mlp_shard = jnp.concatenate([up_weight, down_weight.T], 1)
    mlp_spread = plan.spread(after(mlp_shard, attn_w[-1], x0))
    up_stack = jnp.stack([piece[:, :units] for piece in mlp_spread])
    down_stack = jnp.stack([piece[:, units:] for piece in mlp_spread])

    normed, mixed, w_all = call(
        lambda *refs: mixed_kernel(n_w, shard, *refs),
        [((length, width), BF), ((length, wide3), BF), ((width, width), BF)],
        [ids, x0, x1, x2, x3, row_gain_one, row_shift_one, qkv_bias_j] + attn_w,
        3,
        11,
    )
    g0 = plan.swap_home(after(cotangent, x1))
    up_pieces = plane_pieces(up_stack)

    attended, logs = call(
        attend_kernel,
        [((length, wide), BF), ((8, length), F32)],
        [ids, mixed],
        6,
        10,
    )
    out_t = jnp.stack([piece[..., wide3:] for piece in attn_w])
    out_z = plan.over_z(after(out_t, mixed))
    outs = [out_t, out_z, plan.over_core(out_t), plan.over_core(out_z)]
    att_z = plan.over_z(after(attended, g0, *up_pieces))
    down_pieces = plane_pieces(after(down_stack, attended))
    att_last = after(att_z, *outs, *down_pieces[1:])
    att = [attended, att_z, plan.over_core(attended), plan.over_core(att_last)]

    hidden_own, normed_two, act, slope, up_j = call(
        lambda *refs: forward_kernel(n_w, shard, *refs),
        [
            ((rows, width), F32),
            ((length, width), BF),
            ((length, units), BF),
            ((length, units), BF),
            ((width, units), BF),
        ],
        [ids]
        + att
        + outs
        + [x0, x1, x2, x3]
        + [row(out_bias), row_gain_two, row_shift_two, up_bias_j]
        + up_pieces,
        7,
        22,
        [pltpu.VMEM((4, width, wide), BF)],
    )
    g1 = plan.over_z(after(g0, att_z))
    gs = [g0, g1, plan.over_core(g0), plan.over_core(after(g1, slope))]
    grad_up, gn2_own, gn2_one, gn2_second, up_bias_grad, down_t = call(
        lambda *refs: backward_kernel(n_w, shard, *refs),
        [((length, units), BF)] + parts() + [((1, units), F32), ((width, units), BF)],
        [ids] + down_pieces + gs + [slope, up_j],
        5,
        18,
    )
    gn2_core = plan.over_core(gn2_second)
    gn2_z_in = toward_z(gn2_one, gn2_core)
    gn2_z = plan.over_z(gn2_z_in)
    out_own, out_one, out_second = call(
        mlp_out_kernel,
        parts(),
        [ids, act, down_t],
        2,
        12,
    )
    out_core = plan.over_core(out_second)
    out_z_in = toward_z(out_one, out_core)
    out_here = (hidden_own + out_own + out_core[0].astype(F32) + down_bias).astype(BF)
    mlp_grad = call(
        lambda *refs: mlp_grad_kernel(n_o, shard, *refs),
        grad_outs(2 * units),
        [ids, after(normed_two, gn2_z_in)] + gs + [act, grad_up],
        5,
        22,
        [pltpu.VMEM((width, 2 * units), F32)],
    )
    grad_hidden, gh0, sums_two = call(
        norm_two_kernel,
        [((rows, width), F32), ((rows, width), BF), ((8, width), F32)],
        [ids, gn2_own, gn2_core, gn2_z, after(hidden_own, mlp_grad[-1]), g0, row_gain_two],
        2,
        8,
    )
    gh1 = plan.over_z(gh0)
    mlp_got = plane_got(mlp_grad)
    ghs = [gh0, gh1, plan.over_core(gh0), plan.over_core(after(gh1, *mlp_got[:2]))]
    out_sent = [plan.swap_home(after(out_here, gh1)), plan.swap_next(after(out_z_in, gh1))]
    grad_mixed, gn1_own, gn1_one, gn1_second, small = call(
        attend_back_kernel,
        [((length, wide3), BF)] + parts() + [((16, width), F32)],
        [ids, after(mixed, out_z_in, out_here), logs, w_all]
        + ghs
        + [x0, x1, x2, x3, sums_two, up_bias_grad],
        12,
        22,
        [pltpu.VMEM((length, wide), F32), pltpu.VMEM((length, 3 * HEAD_DIM), F32)],
    )
    gn1_core = plan.over_core(after(gn1_second, *out_sent, *mlp_got[2:]))
    gn1_z_in = toward_z(gn1_one, gn1_core)
    gn1_z = plan.over_z(gn1_z_in)
    mlp_part = plane_total(mlp_grad, mlp_got, gn1_z_in).astype(BF).reshape(2, shard, 2 * units)
    mlp_summed = plan.unspread(mlp_part)
    attn_grad = call(
        lambda *refs: attn_grad_kernel(n_o, shard, *refs),
        grad_outs(width),
        [ids, after(normed, gn1_z_in), grad_mixed] + ghs + [attended],
        3,
        14,
        [pltpu.VMEM((width, width), F32)],
    )
    small = plan.chip_sum(after(small, gn1_z_in))
    (grad_low,) = call(
        norm_one_kernel,
        [((rows, width), BF)],
        [ids, gn1_own, gn1_core, gn1_z, x0, row_gain_one, grad_hidden],
        2,
        12,
    )
    home = plan.swap_home(grad_low)
    attn_grad = lax.optimization_barrier(tuple(attn_grad) + (small,))[:-1]
    attn_got = plane_got(attn_grad)

    attn_total = plane_total(attn_grad, attn_got, home)
    small = after(small, grad_low)
    small = small + plan.over_z(small)
    small = small + plan.over_two(small)
    attn_part = after(attn_total, small).astype(BF).reshape(2, shard, width)
    attn_summed = plan.unspread(attn_part)
    output = (out_sent[0].astype(F32) + out_sent[1].astype(F32)).astype(BF)
    grad_tokens = home.astype(F32)
    mine = lax.dynamic_slice_in_dim(small, 6 + 2 * plan.t, 2, 0)
    return (
        output,
        grad_tokens,
        small[0],
        small[1],
        attn_summed[:, :wide3].reshape(shard, 3, wide),
        mine[0, :wide3].reshape(3, wide),
        attn_summed[:, wide3:].T,
        small[2],
        small[3],
        small[4],
        mlp_summed[:, :units],
        mine[1, :units],
        mlp_summed[:, units:].T,
        small[5],
    )


def solution(mesh):
    in_specs = (
        P(("dp", "tensor"), None),
        P(),
        P(),
        P("dp", None, "tensor"),
        P(None, "tensor"),
        P("tensor", "dp"),
        P(),
        P(),
        P(),
        P("dp", "tensor"),
        P("tensor"),
        P("tensor", "dp"),
        P(),
        P(("dp", "tensor"), None),
    )
    out_specs = (
        P(("dp", "tensor"), None),
        P(("dp", "tensor"), None),
        P(),
        P(),
        P("dp", None, "tensor"),
        P(None, "tensor"),
        P("tensor", "dp"),
        P(),
        P(),
        P(),
        P("dp", "tensor"),
        P("tensor"),
        P("tensor", "dp"),
        P(),
    )
    return jax.shard_map(local, mesh=mesh, in_specs=in_specs, out_specs=out_specs, check_vma=False)
```

```python
import jax
import jax.numpy as jnp
from jax import lax
from jax.experimental import pallas as pl
from jax.experimental.pallas import tpu as pltpu
from jax.sharding import PartitionSpec as P

HEAD_DIM = 64
EPS = 1e-05
BF = jnp.bfloat16
F32 = jnp.float32
AXES = ("dp", "tensor")


def dot_nn(left, right):
    return lax.dot_general(left, right, (((1,), (0,)), ((), ())), preferred_element_type=F32)


def dot_nt(left, right):
    return lax.dot_general(left, right, (((1,), (1,)), ((), ())), preferred_element_type=F32)


def dot_tn(left, right):
    return lax.dot_general(left, right, (((0,), (0,)), ((), ())), preferred_element_type=F32)


class Plan:
    def __init__(self):
        self.n_dp = lax.axis_size("dp")
        self.n_t = lax.axis_size("tensor")
        assert self.n_t == 4 and self.n_dp % 2 == 0
        self.n_k = self.n_dp // 2
        assert self.n_k & (self.n_k - 1) == 0
        self.d = lax.axis_index("dp")
        self.t = lax.axis_index("tensor")
        self.k = self.d // 2
        self.c = self.d % 2
        self.h = self.t // 2
        self.r = jnp.where(self.c == self.h, self.t, self.t ^ 2)
        self.j = self.c + 2 * (self.t % 2)

    def send(self, value, where):
        pairs = []
        for d in range(self.n_dp):
            for t in range(self.n_t):
                to_d, to_t = where(d, t)
                pairs.append((d * self.n_t + t, to_d * self.n_t + to_t))
        return lax.ppermute(value, AXES, pairs)

    def swap_home(self, value):
        return self.send(value, lambda d, t: (d, t) if d % 2 == t // 2 else (d ^ 1, t ^ 2))

    def swap_next(self, value):
        return self.send(value, lambda d, t: (d, t ^ 1) if d % 2 == t // 2 else (d ^ 1, t ^ 3))

    def over_z(self, value):
        return self.send(value, lambda d, t: (d, t ^ 1))

    def over_core(self, value):
        return self.send(value, lambda d, t: (d ^ 1, t))

    def over_plane(self, value, p):
        return self.send(value, lambda d, t: (d ^ (2 * p), t))

    def group_gather(self, value):
        mine = jnp.stack([value, self.over_z(value)])
        return mine, self.over_core(mine)

    def group_sum(self, first, second):
        pair = first + self.over_core(second).astype(F32)
        return pair[0] + self.over_z(pair[1].astype(BF)).astype(F32)

    def spread(self, shard):
        got = []
        for i in (0, 1):
            got.append(
                self.send(
                    shard, lambda d, t, i=i: (2 * (d // 2) + t % 2, t // 2 + 2 * ((d % 2) ^ i))
                )
            )
        return got

    def to_slot(self, value):
        return self.send(value, lambda d, t: (2 * (d // 2) + t % 2, t // 2 + 2 * (d % 2)))

    def unspread(self, chunk):
        total = 0.0
        for i in (0, 1):
            part = lax.dynamic_index_in_dim(chunk, self.h ^ i, 0, keepdims=False)
            got = self.send(
                part, lambda d, t, i=i: (2 * (d // 2) + ((t // 2) ^ i), d % 2 + 2 * (t % 2))
            )
            total = total + got.astype(F32)
        return total

    def plane_gather(self, value):
        if self.n_k == 4:
            return jnp.stack([value] + [self.over_plane(value, p) for p in (1, 2, 3)])
        held = value[None]
        size = 1
        while size < self.n_k:
            held = jnp.concatenate([held, self.over_plane(held, size)])
            size *= 2
        return held

    def plane_sum(self, value):
        pick = lambda p: lax.dynamic_index_in_dim(value, self.k ^ p, 0, keepdims=False)
        if self.n_k == 4:
            total = pick(0).astype(F32)
            for p in (1, 2, 3):
                total = total + self.over_plane(pick(p).astype(BF), p).astype(F32)
            return total
        held = jnp.stack([pick(p) for p in range(self.n_k)]).astype(F32)
        size = self.n_k // 2
        while size:
            held = held[:size] + self.over_plane(held[size:].astype(BF), size).astype(F32)
            size //= 2
        return held[0]

    def ordered_weight(self, held):
        flat = held.reshape((self.n_dp,) + held.shape[2:])
        parts = []
        for d in range(self.n_dp):
            at = ((d // 2) ^ self.k) * 2 + ((d % 2) ^ self.h)
            parts.append(lax.dynamic_index_in_dim(flat, at, 0, keepdims=False))
        return jnp.concatenate(parts, 0)

    def ordered_rows(self, first, second):
        flat = jnp.concatenate([first, second])
        return jnp.concatenate(
            [lax.dynamic_index_in_dim(flat, a ^ self.r, 0, keepdims=False) for a in range(4)], 0
        )

    def relative_rows(self, value):
        rows = value.reshape((4, -1) + value.shape[1:])
        return [lax.dynamic_index_in_dim(rows, i ^ self.r, 0, keepdims=False) for i in range(4)]

    def chip_sum(self, value):
        value = value + self.over_core(value)
        p = 1
        while p < self.n_k:
            value = value + self.over_plane(value, p)
            p *= 2
        return value

    def over_two(self, value):
        return self.send(value, lambda d, t: (d, t ^ 2))


def after(value, *earlier):
    return lax.optimization_barrier((value,) + earlier)[0]


PEAK = 1.15e9


def call(body, outs, args, micros, mib, scratch=()):
    shapes = tuple(jax.ShapeDtypeStruct(shape, dtype) for shape, dtype in outs)
    cost = pl.CostEstimate(
        flops=int(micros * PEAK), bytes_accessed=int(micros * 3.0e6), transcendentals=0
    )

    return pl.pallas_call(
        body,
        out_shape=shapes,
        in_specs=[pl.BlockSpec(memory_space=pltpu.SMEM)]
        + [pl.BlockSpec(memory_space=pltpu.VMEM)] * (len(args) - 1),
        out_specs=tuple(pl.BlockSpec(memory_space=pltpu.VMEM) for _ in shapes),
        scratch_shapes=list(scratch),
        compiler_params=pltpu.CompilerParams(vmem_limit_bytes=mib * 2**20),
        cost_estimate=cost,
    )(*args)


def normalise(values):
    middle = jnp.mean(values, -1, keepdims=True)
    centred = values - middle
    variance = jnp.mean(centred * centred, -1, keepdims=True)
    rate = lax.rsqrt(variance + EPS)
    return centred * rate, rate


def norm_back(grad, hat, rate, gain):
    scaled = grad * gain
    first = jnp.mean(scaled, -1, keepdims=True)
    second = jnp.mean(scaled * hat, -1, keepdims=True)
    return rate * (scaled - first - hat * second)


def col_sum(values):
    return jnp.sum(values, 0, keepdims=True)


def chunk_at(ids, i, rows):
    return pl.ds(pl.multiple_of((ids[2] ^ i) * rows, rows), rows)


def order_weight(ids, pieces, scratch, shard):
    if len(pieces) == 1:
        scratch[...] = pieces[0][0]
        return
    for p, piece in enumerate(pieces):
        for i in range(2):
            at = 2 * (ids[0] ^ p) + (ids[1] ^ i)
            scratch[pl.ds(pl.multiple_of(at * shard, shard), shard), :] = piece[i]


def mixed_kernel(n_w, shard, ids, x0, x1, x2, x3, gain, shift, bias, *refs):
    pieces, (normed, mixed, w_all) = refs[:n_w], refs[n_w:]
    order_weight(ids, pieces, w_all, shard)
    wide = mixed.shape[1]
    for i, x in enumerate((x0, x1, x2, x3)):
        rows = x.shape[0]
        hat, _ = normalise(x[...].astype(F32))
        low = (hat * gain[...] + shift[...]).astype(BF)
        normed[chunk_at(ids, i, rows), :] = low
        out = dot_nn(low, w_all[:, :wide]) + bias[...]
        mixed[chunk_at(ids, i, rows), :] = out.astype(BF)


def attend_kernel(ids, mixed, attended, logs):
    length, wide = attended.shape
    block = min(512, length)
    tri = lax.broadcasted_iota(jnp.int32, (block, block), 0) <= lax.broadcasted_iota(
        jnp.int32, (block, block), 1
    )
    for head in range(wide // HEAD_DIM):
        at = head * HEAD_DIM
        q_t = (mixed[:, at : at + HEAD_DIM].astype(F32) * HEAD_DIM ** (-0.5)).T.astype(BF)
        keys = mixed[:, wide + at : wide + at + HEAD_DIM]
        v_t = mixed[:, 2 * wide + at : 2 * wide + at + HEAD_DIM].astype(F32).T.astype(BF)
        for b in range(length // block):
            low = b * block
            q_b = q_t[:, low : low + block]
            near = jnp.where(tri, dot_nn(keys[low : low + block], q_b), -1e30)
            top = jnp.max(near, 0, keepdims=True)
            if b:
                far = dot_nn(keys[:low], q_b)
                top = jnp.maximum(top, jnp.max(far, 0, keepdims=True))
            near = jnp.exp(near - top)
            total = col_sum(near)
            out = dot_nn(v_t[:, low : low + block], near.astype(BF))
            if b:
                far = jnp.exp(far - top)
                total = total + col_sum(far)
                out = out + dot_nn(v_t[:, :low], far.astype(BF))
            out = out * (1.0 / total)
            attended[low : low + block, at : at + HEAD_DIM] = out.T.astype(BF)
            logs[head : head + 1, low : low + block] = top + jnp.log(total)


def forward_kernel(n_w, shard, ids, *refs):
    att, outs, xs = refs[0:4], refs[4:8], refs[8:12]
    out_bias, gain, shift, up_bias = refs[12:16]
    pieces = refs[16 : 16 + n_w]
    hidden_own, normed_two, act, slope, up_w = refs[16 + n_w : 21 + n_w]
    out_w = refs[21 + n_w]
    order_weight(ids, pieces, up_w, shard)
    for g, out in enumerate(outs):
        if n_w == 1:
            out_w[g] = out[0, 0]
        else:
            for p in range(n_w):
                for i in range(2):
                    at = 2 * (ids[0] ^ p) + (ids[1] ^ i)
                    out_w[g, pl.ds(pl.multiple_of(at * shard, shard), shard), :] = out[p, i]
    for i in range(4):
        rows = xs[0].shape[0]
        hidden = xs[i][...].astype(F32) + out_bias[...]
        for g in range(4):
            hidden = hidden + dot_nt(att[g][chunk_at(ids, i, rows), :], out_w[g])
        if i == 0:
            hidden_own[...] = hidden
        hat, _ = normalise(hidden)
        low = (hat * gain[...] + shift[...]).astype(BF)
        span = slice(i * rows, (i + 1) * rows)
        normed_two[span, :] = low
        up = dot_nn(low, up_w[...]) + up_bias[...]
        whole = 0.5 * (1.0 + lax.erf(up * 0.5**0.5))
        act[span, :] = (up * whole).astype(BF)
        bell = jnp.exp(-0.5 * up * up) * (2.0 * jnp.pi) ** (-0.5)
        slope[span, :] = (whole + up * bell).astype(BF)


def backward_kernel(n_w, shard, ids, *refs):
    pieces = refs[:n_w]
    g0, g1, g2, g3, slope, up_w = refs[n_w : n_w + 6]
    grad_up, own, after_one, second, bias_grad, down_t = refs[n_w + 6 :]
    rows = g0.shape[0]
    units = slope.shape[1]
    order_weight(ids, pieces, down_t, shard)
    bias_sum = jnp.zeros((1, units), F32)
    for i, g in enumerate((g0, g1, g2, g3)):
        span = slice(i * rows, (i + 1) * rows)
        grad = (dot_nn(g[...], down_t[...]) * slope[span, :].astype(F32)).astype(BF)
        grad_up[span, :] = grad
        bias_sum = bias_sum + col_sum(grad.astype(F32))
        put_part(i, dot_nt(grad, up_w[...]), own, after_one, second)
    bias_grad[...] = bias_sum


def put_part(i, value, own, after_one, second):
    if i == 0:
        own[...] = value
    elif i == 1:
        after_one[...] = value
    else:
        second[i - 2] = value.astype(BF)


def mlp_grad_kernel(n_o, shard, ids, normed_two, g0, g1, g2, g3, act, grad_up, *refs):
    outs, scratch = refs[:n_o], refs[n_o]
    units = act.shape[1]
    rows = g0.shape[0]
    scratch[:, :units] = dot_tn(normed_two[...], grad_up[...])
    total = 0.0
    for i, g in enumerate((g0, g1, g2, g3)):
        total = total + dot_tn(g[...], act[i * rows : (i + 1) * rows, :])
    scratch[:, units:] = total
    emit_grad(ids, scratch, outs, shard)


def emit_grad(ids, scratch, outs, shard):
    if len(outs) == 1:
        outs[0][...] = scratch[...]
        return
    for p, out in enumerate(outs):
        at = pl.ds(pl.multiple_of((ids[0] ^ p) * 2 * shard, 2 * shard), 2 * shard)
        out[...] = scratch[at, :].astype(out.dtype)


def mlp_out_kernel(ids, act, down_t, own, after_one, second):
    rows = own.shape[0]
    for i in range(4):
        out = dot_nt(act[i * rows : (i + 1) * rows, :], down_t[...])
        put_part(i, out, own, after_one, second)


def norm_two_kernel(ids, own, got_core, got_z, hidden, g, gain, grad_hidden, low, sums):
    grad = own[...] + got_core[0].astype(F32) + got_z[...].astype(F32)
    hat, rate = normalise(hidden[...])
    g32 = g[...].astype(F32)
    total = g32 + norm_back(grad, hat, rate, gain[...])
    grad_hidden[...] = total
    low[...] = total.astype(BF)
    sums[0:1, :] = col_sum(total)
    sums[1:2, :] = col_sum(grad * hat)
    sums[2:3, :] = col_sum(grad)
    sums[3:4, :] = col_sum(g32)


def norm_one_kernel(ids, own, got_core, got_z, x, gain, grad_hidden, out):
    grad = own[...] + got_core[0].astype(F32) + got_z[...].astype(F32)
    hat, rate = normalise(x[...].astype(F32))
    total = grad_hidden[...] + norm_back(grad, hat, rate, gain[...])
    out[...] = total.astype(BF)


def attend_back_kernel(ids, mixed, logs, w_all, gh0, gh1, gh2, gh3, x0, x1, x2, x3, *refs):
    sums_two, up_bias, grad_mixed, own, after_one, second, small, g_rows, gm32 = refs
    length, wide3 = mixed.shape
    wide = wide3 // 3
    rows = x0.shape[0]
    block = min(512, length)
    for i, gh in enumerate((gh0, gh1, gh2, gh3)):
        g_rows[chunk_at(ids, i, rows), :] = dot_nn(gh[...], w_all[:, wide3:])
    tri = lax.broadcasted_iota(jnp.int32, (block, block), 0) <= lax.broadcasted_iota(
        jnp.int32, (block, block), 1
    )
    for head in range(wide // HEAD_DIM):
        at = head * HEAD_DIM
        scaled = mixed[:, at : at + HEAD_DIM].astype(F32) * HEAD_DIM ** (-0.5)
        q_rows = scaled.astype(BF)
        q_t = scaled.T.astype(BF)
        keys = mixed[:, wide + at : wide + at + HEAD_DIM]
        k_t = keys.astype(F32).T.astype(BF)
        values = mixed[:, 2 * wide + at : 2 * wide + at + HEAD_DIM]
        grad32 = g_rows[:, at : at + HEAD_DIM]
        grad_rows = grad32.astype(BF)
        grad_t = grad32.T.astype(BF)
        for b in range(length // block):
            low, end = b * block, (b + 1) * block
            q_b = q_t[:, low:end]
            g_b = grad_t[:, low:end]
            log = logs[head : head + 1, low:end]
            near = jnp.where(tri, jnp.exp(dot_nn(keys[low:end], q_b) - log), 0.0)
            near_d = dot_nn(values[low:end], g_b)
            inner = col_sum(near * near_d)
            if b:
                far = jnp.exp(dot_nn(keys[:low], q_b) - log)
                far_d = dot_nn(values[:low], g_b)
                inner = inner + col_sum(far * far_d)
            near_s = (near * (near_d - inner)).astype(BF)
            grad_q = dot_nn(k_t[:, low:end], near_s)
            gm32[low:end, HEAD_DIM : 2 * HEAD_DIM] = dot_nn(near_s, q_rows[low:end])
            gm32[low:end, 2 * HEAD_DIM :] = dot_nn(near.astype(BF), grad_rows[low:end])
            if b:
                far_s = (far * (far_d - inner)).astype(BF)
                grad_q = grad_q + dot_nn(k_t[:, :low], far_s)
                gm32[:low, HEAD_DIM : 2 * HEAD_DIM] += dot_nn(far_s, q_rows[low:end])
                gm32[:low, 2 * HEAD_DIM :] += dot_nn(far.astype(BF), grad_rows[low:end])
            gm32[low:end, :HEAD_DIM] = grad_q.T * HEAD_DIM ** (-0.5)
        for part in range(3):
            grad_mixed[:, part * wide + at : part * wide + at + HEAD_DIM] = gm32[
                :, part * HEAD_DIM : (part + 1) * HEAD_DIM
            ].astype(BF)
    bias_grad = col_sum(grad_mixed[...].astype(F32))
    gain_sum = jnp.zeros((1, x0.shape[1]), F32)
    shift_sum = gain_sum
    for i, x in enumerate((x0, x1, x2, x3)):
        back = dot_nt(grad_mixed[chunk_at(ids, i, rows), :], w_all[:, :wide3])
        hat, _ = normalise(x[...].astype(F32))
        gain_sum = gain_sum + col_sum(back * hat)
        shift_sum = shift_sum + col_sum(back)
        put_part(i, back, own, after_one, second)
    small[...] = jnp.zeros(small.shape, F32)
    small[0:1, :] = gain_sum
    small[1:2, :] = shift_sum
    small[2:6, :] = sums_two[0:4, :]
    small[pl.ds(6 + 2 * ids[3], 1), :wide3] = bias_grad
    small[pl.ds(7 + 2 * ids[3], 1), : up_bias.shape[1]] = up_bias[...]


def attn_grad_kernel(n_o, shard, ids, normed, grad_mixed, gh0, gh1, gh2, gh3, attended, *refs):
    outs, scratch = refs[:n_o], refs[n_o]
    wide3 = grad_mixed.shape[1]
    rows = gh0.shape[0]
    scratch[:, :wide3] = dot_tn(normed[...], grad_mixed[...])
    total = 0.0
    for i, gh in enumerate((gh0, gh1, gh2, gh3)):
        total = total + dot_tn(gh[...], attended[chunk_at(ids, i, rows), :])
    scratch[:, wide3:] = total
    emit_grad(ids, scratch, outs, shard)


def local(
    tokens,
    gain_one,
    shift_one,
    qkv_weight,
    qkv_bias,
    out_weight,
    out_bias,
    gain_two,
    shift_two,
    up_weight,
    up_bias,
    down_weight,
    down_bias,
    cotangent,
):
    plan = Plan()
    rows, width = tokens.shape
    shard = qkv_weight.shape[0]
    wide = qkv_weight.shape[2]
    wide3 = 3 * wide
    units = up_weight.shape[1]
    length = 4 * rows
    n_k = plan.n_k
    direct = n_k == 4 and shard % 16 == 0
    n_w = n_k if direct else 1
    n_o = n_k if direct else 1
    ids = jnp.stack([plan.k, plan.h, plan.r, plan.j]).astype(jnp.int32)
    row = lambda v: v.reshape(1, -1)
    row_gain_one, row_shift_one = row(gain_one), row(shift_one)
    row_gain_two, row_shift_two = row(gain_two), row(shift_two)

    def plane_pieces(value):
        if direct:
            return [value] + [plan.over_plane(value, p) for p in (1, 2, 3)]
        return [plan.ordered_weight(plan.plane_gather(value))[None]]

    def plane_got(pieces):
        return [plan.over_plane(pieces[p], p) for p in (1, 2, 3)] if direct else []

    def plane_total(pieces, got, *earlier):
        if direct:
            total = after(pieces[0], *earlier)
            for value in got:
                total = total + value.astype(F32)
            return total
        return plan.plane_sum(pieces[0].reshape((n_k, 2 * shard) + pieces[0].shape[1:]))

    def grad_outs(n):
        if direct:
            return [((2 * shard, n), F32)] + [((2 * shard, n), BF)] * (n_k - 1)
        return [((width, n), F32)]

    def parts():
        return [((rows, width), F32), ((rows, width), F32), ((2, rows, width), BF)]

    def toward_z(after_one, got_core):
        return (after_one + got_core[1].astype(F32)).astype(BF)

    x0 = plan.swap_home(tokens)
    attn_shard = jnp.concatenate([qkv_weight.reshape(shard, wide3), out_weight.T], 1)
    attn_spread = jnp.stack(plan.spread(attn_shard))
    biases = plan.to_slot(jnp.concatenate([qkv_bias.reshape(-1), up_bias]))
    qkv_bias_j, up_bias_j = row(biases[:wide3]), row(biases[wide3:])
    x1 = plan.over_z(x0)
    x2 = plan.over_core(x0)
    x3 = plan.over_core(x1)
    attn_w = plane_pieces(attn_spread)

    mlp_shard = jnp.concatenate([up_weight, down_weight.T], 1)
    mlp_spread = plan.spread(after(mlp_shard, attn_w[-1], x0))
    up_stack = jnp.stack([piece[:, :units] for piece in mlp_spread])
    down_stack = jnp.stack([piece[:, units:] for piece in mlp_spread])

    normed, mixed, w_all = call(
        lambda *refs: mixed_kernel(n_w, shard, *refs),
        [((length, width), BF), ((length, wide3), BF), ((width, width), BF)],
        [ids, x0, x1, x2, x3, row_gain_one, row_shift_one, qkv_bias_j] + attn_w,
        3,
        11,
    )
    g0 = plan.swap_home(after(cotangent, x1))
    up_pieces = plane_pieces(up_stack)

    attended, logs = call(
        attend_kernel,
        [((length, wide), BF), ((8, length), F32)],
        [ids, mixed],
        6,
        10,
    )
    out_t = jnp.stack([piece[..., wide3:] for piece in attn_w])
    out_z = plan.over_z(after(out_t, mixed))
    outs = [out_t, out_z, plan.over_core(out_t), plan.over_core(out_z)]
    att_z = plan.over_z(after(attended, g0, *up_pieces))
    down_pieces = plane_pieces(after(down_stack, attended))
    att_last = after(att_z, *outs, *down_pieces[1:])
    att = [attended, att_z, plan.over_core(attended), plan.over_core(att_last)]

    hidden_own, normed_two, act, slope, up_j = call(
        lambda *refs: forward_kernel(n_w, shard, *refs),
        [
            ((rows, width), F32),
            ((length, width), BF),
            ((length, units), BF),
            ((length, units), BF),
            ((width, units), BF),
        ],
        [ids]
        + att
        + outs
        + [x0, x1, x2, x3]
        + [row(out_bias), row_gain_two, row_shift_two, up_bias_j]
        + up_pieces,
        7,
        22,
        [pltpu.VMEM((4, width, wide), BF)],
    )
    g1 = plan.over_z(after(g0, att_z))
    gs = [g0, g1, plan.over_core(g0), plan.over_core(after(g1, slope))]
    grad_up, gn2_own, gn2_one, gn2_second, up_bias_grad, down_t = call(
        lambda *refs: backward_kernel(n_w, shard, *refs),
        [((length, units), BF)] + parts() + [((1, units), F32), ((width, units), BF)],
        [ids] + down_pieces + gs + [slope, up_j],
        5,
        18,
    )
    gn2_core = plan.over_core(gn2_second)
    gn2_z_in = toward_z(gn2_one, gn2_core)
    gn2_z = plan.over_z(gn2_z_in)
    out_own, out_one, out_second = call(
        mlp_out_kernel,
        parts(),
        [ids, act, down_t],
        2,
        12,
    )
    out_core = plan.over_core(out_second)
    out_z_in = toward_z(out_one, out_core)
    out_here = (hidden_own + out_own + out_core[0].astype(F32) + down_bias).astype(BF)
    mlp_grad = call(
        lambda *refs: mlp_grad_kernel(n_o, shard, *refs),
        grad_outs(2 * units),
        [ids, after(normed_two, gn2_z_in)] + gs + [act, grad_up],
        5,
        22,
        [pltpu.VMEM((width, 2 * units), F32)],
    )
    grad_hidden, gh0, sums_two = call(
        norm_two_kernel,
        [((rows, width), F32), ((rows, width), BF), ((8, width), F32)],
        [ids, gn2_own, gn2_core, gn2_z, after(hidden_own, mlp_grad[-1]), g0, row_gain_two],
        2,
        8,
    )
    gh1 = plan.over_z(gh0)
    mlp_got = plane_got(mlp_grad)
    ghs = [gh0, gh1, plan.over_core(gh0), plan.over_core(after(gh1, *mlp_got[:2]))]
    out_sent = [plan.swap_home(after(out_here, gh1)), plan.swap_next(after(out_z_in, gh1))]
    grad_mixed, gn1_own, gn1_one, gn1_second, small = call(
        attend_back_kernel,
        [((length, wide3), BF)] + parts() + [((16, width), F32)],
        [ids, after(mixed, out_z_in, out_here), logs, w_all]
        + ghs
        + [x0, x1, x2, x3, sums_two, up_bias_grad],
        12,
        22,
        [pltpu.VMEM((length, wide), F32), pltpu.VMEM((length, 3 * HEAD_DIM), F32)],
    )
    gn1_core = plan.over_core(after(gn1_second, *out_sent, *mlp_got[2:]))
    gn1_z_in = toward_z(gn1_one, gn1_core)
    gn1_z = plan.over_z(gn1_z_in)
    mlp_part = plane_total(mlp_grad, mlp_got, gn1_z_in).astype(BF).reshape(2, shard, 2 * units)
    mlp_summed = plan.unspread(mlp_part)
    attn_grad = call(
        lambda *refs: attn_grad_kernel(n_o, shard, *refs),
        grad_outs(width),
        [ids, after(normed, gn1_z_in), grad_mixed] + ghs + [attended],
        3,
        14,
        [pltpu.VMEM((width, width), F32)],
    )
    small = plan.chip_sum(after(small, gn1_z_in))
    (grad_low,) = call(
        norm_one_kernel,
        [((rows, width), BF)],
        [ids, gn1_own, gn1_core, gn1_z, after(x0, attn_grad[-1]), row_gain_one, grad_hidden],
        2,
        12,
    )
    home = plan.swap_home(grad_low)
    attn_grad = lax.optimization_barrier(tuple(attn_grad) + (small,))[:-1]
    attn_got = plane_got(attn_grad)

    attn_total = plane_total(attn_grad, attn_got, home)
    small = after(small, grad_low)
    small = small + plan.over_z(small)
    attn_part = after(attn_total, small).astype(BF).reshape(2, shard, width)
    small = small + plan.over_two(small)
    attn_summed = plan.unspread(attn_part)
    output = (out_sent[0].astype(F32) + out_sent[1].astype(F32)).astype(BF)
    grad_tokens = home.astype(F32)
    mine = lax.dynamic_slice_in_dim(small, 6 + 2 * plan.t, 2, 0)
    return (
        output,
        grad_tokens,
        small[0],
        small[1],
        attn_summed[:, :wide3].reshape(shard, 3, wide),
        mine[0, :wide3].reshape(3, wide),
        attn_summed[:, wide3:].T,
        small[2],
        small[3],
        small[4],
        mlp_summed[:, :units],
        mine[1, :units],
        mlp_summed[:, units:].T,
        small[5],
    )


def solution(mesh):
    in_specs = (
        P(("dp", "tensor"), None),
        P(),
        P(),
        P("dp", None, "tensor"),
        P(None, "tensor"),
        P("tensor", "dp"),
        P(),
        P(),
        P(),
        P("dp", "tensor"),
        P("tensor"),
        P("tensor", "dp"),
        P(),
        P(("dp", "tensor"), None),
    )
    out_specs = (
        P(("dp", "tensor"), None),
        P(("dp", "tensor"), None),
        P(),
        P(),
        P("dp", None, "tensor"),
        P(None, "tensor"),
        P("tensor", "dp"),
        P(),
        P(),
        P(),
        P("dp", "tensor"),
        P("tensor"),
        P("tensor", "dp"),
        P(),
    )
    return jax.shard_map(local, mesh=mesh, in_specs=in_specs, out_specs=out_specs, check_vma=False)
```

```python
import jax
import jax.numpy as jnp
from jax import lax
from jax.experimental import pallas as pl
from jax.experimental.pallas import tpu as pltpu
from jax.sharding import PartitionSpec as P

HEAD_DIM = 64
EPS = 1e-05
BF = jnp.bfloat16
F32 = jnp.float32
AXES = ("dp", "tensor")


def dot_nn(left, right):
    return lax.dot_general(left, right, (((1,), (0,)), ((), ())), preferred_element_type=F32)


def dot_nt(left, right):
    return lax.dot_general(left, right, (((1,), (1,)), ((), ())), preferred_element_type=F32)


def dot_tn(left, right):
    return lax.dot_general(left, right, (((0,), (0,)), ((), ())), preferred_element_type=F32)


class Plan:
    def __init__(self):
        self.n_dp = lax.axis_size("dp")
        self.n_t = lax.axis_size("tensor")
        assert self.n_t == 4 and self.n_dp % 2 == 0
        self.n_k = self.n_dp // 2
        assert self.n_k & (self.n_k - 1) == 0
        self.d = lax.axis_index("dp")
        self.t = lax.axis_index("tensor")
        self.k = self.d // 2
        self.c = self.d % 2
        self.h = self.t // 2
        self.r = jnp.where(self.c == self.h, self.t, self.t ^ 2)
        self.j = self.c + 2 * (self.t % 2)

    def send(self, value, where):
        pairs = []
        for d in range(self.n_dp):
            for t in range(self.n_t):
                to_d, to_t = where(d, t)
                pairs.append((d * self.n_t + t, to_d * self.n_t + to_t))
        return lax.ppermute(value, AXES, pairs)

    def swap_home(self, value):
        return self.send(value, lambda d, t: (d, t) if d % 2 == t // 2 else (d ^ 1, t ^ 2))

    def swap_next(self, value):
        return self.send(value, lambda d, t: (d, t ^ 1) if d % 2 == t // 2 else (d ^ 1, t ^ 3))

    def over_z(self, value):
        return self.send(value, lambda d, t: (d, t ^ 1))

    def over_core(self, value):
        return self.send(value, lambda d, t: (d ^ 1, t))

    def over_plane(self, value, p):
        return self.send(value, lambda d, t: (d ^ (2 * p), t))

    def group_gather(self, value):
        mine = jnp.stack([value, self.over_z(value)])
        return mine, self.over_core(mine)

    def group_sum(self, first, second):
        pair = first + self.over_core(second).astype(F32)
        return pair[0] + self.over_z(pair[1].astype(BF)).astype(F32)

    def spread(self, shard):
        got = []
        for i in (0, 1):
            got.append(
                self.send(
                    shard, lambda d, t, i=i: (2 * (d // 2) + t % 2, t // 2 + 2 * ((d % 2) ^ i))
                )
            )
        return got

    def to_slot(self, value):
        return self.send(value, lambda d, t: (2 * (d // 2) + t % 2, t // 2 + 2 * (d % 2)))

    def unspread(self, chunk):
        total = 0.0
        for i in (0, 1):
            part = lax.dynamic_index_in_dim(chunk, self.h ^ i, 0, keepdims=False)
            got = self.send(
                part, lambda d, t, i=i: (2 * (d // 2) + ((t // 2) ^ i), d % 2 + 2 * (t % 2))
            )
            total = total + got.astype(F32)
        return total

    def plane_gather(self, value):
        if self.n_k == 4:
            return jnp.stack([value] + [self.over_plane(value, p) for p in (1, 2, 3)])
        held = value[None]
        size = 1
        while size < self.n_k:
            held = jnp.concatenate([held, self.over_plane(held, size)])
            size *= 2
        return held

    def plane_sum(self, value):
        pick = lambda p: lax.dynamic_index_in_dim(value, self.k ^ p, 0, keepdims=False)
        if self.n_k == 4:
            total = pick(0).astype(F32)
            for p in (1, 2, 3):
                total = total + self.over_plane(pick(p).astype(BF), p).astype(F32)
            return total
        held = jnp.stack([pick(p) for p in range(self.n_k)]).astype(F32)
        size = self.n_k // 2
        while size:
            held = held[:size] + self.over_plane(held[size:].astype(BF), size).astype(F32)
            size //= 2
        return held[0]

    def ordered_weight(self, held):
        flat = held.reshape((self.n_dp,) + held.shape[2:])
        parts = []
        for d in range(self.n_dp):
            at = ((d // 2) ^ self.k) * 2 + ((d % 2) ^ self.h)
            parts.append(lax.dynamic_index_in_dim(flat, at, 0, keepdims=False))
        return jnp.concatenate(parts, 0)

    def ordered_rows(self, first, second):
        flat = jnp.concatenate([first, second])
        return jnp.concatenate(
            [lax.dynamic_index_in_dim(flat, a ^ self.r, 0, keepdims=False) for a in range(4)], 0
        )

    def relative_rows(self, value):
        rows = value.reshape((4, -1) + value.shape[1:])
        return [lax.dynamic_index_in_dim(rows, i ^ self.r, 0, keepdims=False) for i in range(4)]

    def chip_sum(self, value):
        value = value + self.over_core(value)
        p = 1
        while p < self.n_k:
            value = value + self.over_plane(value, p)
            p *= 2
        return value

    def over_two(self, value):
        return self.send(value, lambda d, t: (d, t ^ 2))


def after(value, *earlier):
    return lax.optimization_barrier((value,) + earlier)[0]


PEAK = 1.15e9


def call(body, outs, args, micros, mib, scratch=()):
    shapes = tuple(jax.ShapeDtypeStruct(shape, dtype) for shape, dtype in outs)
    cost = pl.CostEstimate(
        flops=int(micros * PEAK), bytes_accessed=int(micros * 3.0e6), transcendentals=0
    )

    return pl.pallas_call(
        body,
        out_shape=shapes,
        in_specs=[pl.BlockSpec(memory_space=pltpu.SMEM)]
        + [pl.BlockSpec(memory_space=pltpu.VMEM)] * (len(args) - 1),
        out_specs=tuple(pl.BlockSpec(memory_space=pltpu.VMEM) for _ in shapes),
        scratch_shapes=list(scratch),
        compiler_params=pltpu.CompilerParams(vmem_limit_bytes=mib * 2**20),
        cost_estimate=cost,
    )(*args)


def normalise(values):
    middle = jnp.mean(values, -1, keepdims=True)
    centred = values - middle
    variance = jnp.mean(centred * centred, -1, keepdims=True)
    rate = lax.rsqrt(variance + EPS)
    return centred * rate, rate


def norm_back(grad, hat, rate, gain):
    scaled = grad * gain
    first = jnp.mean(scaled, -1, keepdims=True)
    second = jnp.mean(scaled * hat, -1, keepdims=True)
    return rate * (scaled - first - hat * second)


def col_sum(values):
    return jnp.sum(values, 0, keepdims=True)


def chunk_at(ids, i, rows):
    return pl.ds(pl.multiple_of((ids[2] ^ i) * rows, rows), rows)


def order_weight(ids, pieces, scratch, shard):
    if len(pieces) == 1:
        scratch[...] = pieces[0][0]
        return
    for p, piece in enumerate(pieces):
        for i in range(2):
            at = 2 * (ids[0] ^ p) + (ids[1] ^ i)
            scratch[pl.ds(pl.multiple_of(at * shard, shard), shard), :] = piece[i]


def mixed_kernel(n_w, shard, ids, x0, x1, x2, x3, gain, shift, bias, *refs):
    pieces, (normed, mixed, w_all) = refs[:n_w], refs[n_w:]
    order_weight(ids, pieces, w_all, shard)
    wide = mixed.shape[1]
    for i, x in enumerate((x0, x1, x2, x3)):
        rows = x.shape[0]
        hat, _ = normalise(x[...].astype(F32))
        low = (hat * gain[...] + shift[...]).astype(BF)
        normed[chunk_at(ids, i, rows), :] = low
        out = dot_nn(low, w_all[:, :wide]) + bias[...]
        mixed[chunk_at(ids, i, rows), :] = out.astype(BF)


def attend_kernel(ids, mixed, attended, logs):
    length, wide = attended.shape
    block = min(512, length)
    tri = lax.broadcasted_iota(jnp.int32, (block, block), 0) <= lax.broadcasted_iota(
        jnp.int32, (block, block), 1
    )
    for head in range(wide // HEAD_DIM):
        at = head * HEAD_DIM
        q_t = (mixed[:, at : at + HEAD_DIM].astype(F32) * HEAD_DIM ** (-0.5)).T.astype(BF)
        keys = mixed[:, wide + at : wide + at + HEAD_DIM]
        v_t = mixed[:, 2 * wide + at : 2 * wide + at + HEAD_DIM].astype(F32).T.astype(BF)
        for b in range(length // block):
            low = b * block
            q_b = q_t[:, low : low + block]
            near = jnp.where(tri, dot_nn(keys[low : low + block], q_b), -1e30)
            top = jnp.max(near, 0, keepdims=True)
            if b:
                far = dot_nn(keys[:low], q_b)
                top = jnp.maximum(top, jnp.max(far, 0, keepdims=True))
            near = jnp.exp(near - top)
            total = col_sum(near)
            out = dot_nn(v_t[:, low : low + block], near.astype(BF))
            if b:
                far = jnp.exp(far - top)
                total = total + col_sum(far)
                out = out + dot_nn(v_t[:, :low], far.astype(BF))
            out = out * (1.0 / total)
            attended[low : low + block, at : at + HEAD_DIM] = out.T.astype(BF)
            logs[head : head + 1, low : low + block] = top + jnp.log(total)


def forward_kernel(n_w, shard, ids, *refs):
    att, outs, xs = refs[0:4], refs[4:8], refs[8:12]
    out_bias, gain, shift, up_bias = refs[12:16]
    pieces = refs[16 : 16 + n_w]
    hidden_own, normed_two, act, slope, up_w = refs[16 + n_w : 21 + n_w]
    out_w = refs[21 + n_w]
    order_weight(ids, pieces, up_w, shard)
    for g, out in enumerate(outs):
        if n_w == 1:
            out_w[g] = out[0, 0]
        else:
            for p in range(n_w):
                for i in range(2):
                    at = 2 * (ids[0] ^ p) + (ids[1] ^ i)
                    out_w[g, pl.ds(pl.multiple_of(at * shard, shard), shard), :] = out[p, i]
    for i in range(4):
        rows = xs[0].shape[0]
        hidden = xs[i][...].astype(F32) + out_bias[...]
        for g in range(4):
            hidden = hidden + dot_nt(att[g][chunk_at(ids, i, rows), :], out_w[g])
        if i == 0:
            hidden_own[...] = hidden
        hat, _ = normalise(hidden)
        low = (hat * gain[...] + shift[...]).astype(BF)
        span = slice(i * rows, (i + 1) * rows)
        normed_two[span, :] = low
        up = dot_nn(low, up_w[...]) + up_bias[...]
        whole = 0.5 * (1.0 + lax.erf(up * 0.5**0.5))
        act[span, :] = (up * whole).astype(BF)
        bell = jnp.exp(-0.5 * up * up) * (2.0 * jnp.pi) ** (-0.5)
        slope[span, :] = (whole + up * bell).astype(BF)


def backward_kernel(n_w, shard, ids, *refs):
    pieces = refs[:n_w]
    g0, g1, g2, g3, slope, up_w = refs[n_w : n_w + 6]
    grad_up, own, after_one, second, bias_grad, down_t = refs[n_w + 6 :]
    rows = g0.shape[0]
    units = slope.shape[1]
    order_weight(ids, pieces, down_t, shard)
    bias_sum = jnp.zeros((1, units), F32)
    for i, g in enumerate((g0, g1, g2, g3)):
        span = slice(i * rows, (i + 1) * rows)
        grad = (dot_nn(g[...], down_t[...]) * slope[span, :].astype(F32)).astype(BF)
        grad_up[span, :] = grad
        bias_sum = bias_sum + col_sum(grad.astype(F32))
        put_part(i, dot_nt(grad, up_w[...]), own, after_one, second)
    bias_grad[...] = bias_sum


def put_part(i, value, own, after_one, second):
    if i == 0:
        own[...] = value
    elif i == 1:
        after_one[...] = value
    else:
        second[i - 2] = value.astype(BF)


def mlp_grad_kernel(n_o, shard, ids, normed_two, g0, g1, g2, g3, act, grad_up, *refs):
    outs, scratch = refs[:n_o], refs[n_o]
    units = act.shape[1]
    rows = g0.shape[0]
    scratch[:, :units] = dot_tn(normed_two[...], grad_up[...])
    total = 0.0
    for i, g in enumerate((g0, g1, g2, g3)):
        total = total + dot_tn(g[...], act[i * rows : (i + 1) * rows, :])
    scratch[:, units:] = total
    emit_grad(ids, scratch, outs, shard)


def emit_grad(ids, scratch, outs, shard):
    if len(outs) == 1:
        outs[0][...] = scratch[...]
        return
    for p, out in enumerate(outs):
        at = pl.ds(pl.multiple_of((ids[0] ^ p) * 2 * shard, 2 * shard), 2 * shard)
        out[...] = scratch[at, :].astype(out.dtype)


def mlp_out_kernel(ids, act, down_t, own, after_one, second):
    rows = own.shape[0]
    for i in range(4):
        out = dot_nt(act[i * rows : (i + 1) * rows, :], down_t[...])
        put_part(i, out, own, after_one, second)


def norm_two_kernel(ids, own, got_core, got_z, hidden, g, gain, grad_hidden, low, sums):
    grad = own[...] + got_core[0].astype(F32) + got_z[...].astype(F32)
    hat, rate = normalise(hidden[...])
    g32 = g[...].astype(F32)
    total = g32 + norm_back(grad, hat, rate, gain[...])
    grad_hidden[...] = total
    low[...] = total.astype(BF)
    sums[0:1, :] = col_sum(total)
    sums[1:2, :] = col_sum(grad * hat)
    sums[2:3, :] = col_sum(grad)
    sums[3:4, :] = col_sum(g32)


def norm_one_kernel(ids, own, got_core, got_z, x, gain, grad_hidden, out):
    grad = own[...] + got_core[0].astype(F32) + got_z[...].astype(F32)
    hat, rate = normalise(x[...].astype(F32))
    total = grad_hidden[...] + norm_back(grad, hat, rate, gain[...])
    out[...] = total.astype(BF)


def attend_back_kernel(ids, mixed, logs, w_all, gh0, gh1, gh2, gh3, x0, x1, x2, x3, *refs):
    sums_two, up_bias, grad_mixed, own, after_one, second, small, g_rows, gm32 = refs
    length, wide3 = mixed.shape
    wide = wide3 // 3
    rows = x0.shape[0]
    block = min(512, length)
    for i, gh in enumerate((gh0, gh1, gh2, gh3)):
        g_rows[chunk_at(ids, i, rows), :] = dot_nn(gh[...], w_all[:, wide3:])
    tri = lax.broadcasted_iota(jnp.int32, (block, block), 0) <= lax.broadcasted_iota(
        jnp.int32, (block, block), 1
    )
    for head in range(wide // HEAD_DIM):
        at = head * HEAD_DIM
        scaled = mixed[:, at : at + HEAD_DIM].astype(F32) * HEAD_DIM ** (-0.5)
        q_rows = scaled.astype(BF)
        q_t = scaled.T.astype(BF)
        keys = mixed[:, wide + at : wide + at + HEAD_DIM]
        k_t = keys.astype(F32).T.astype(BF)
        values = mixed[:, 2 * wide + at : 2 * wide + at + HEAD_DIM]
        grad32 = g_rows[:, at : at + HEAD_DIM]
        grad_rows = grad32.astype(BF)
        grad_t = grad32.T.astype(BF)
        for b in range(length // block):
            low, end = b * block, (b + 1) * block
            q_b = q_t[:, low:end]
            g_b = grad_t[:, low:end]
            log = logs[head : head + 1, low:end]
            near = jnp.where(tri, jnp.exp(dot_nn(keys[low:end], q_b) - log), 0.0)
            near_d = dot_nn(values[low:end], g_b)
            inner = col_sum(near * near_d)
            if b:
                far = jnp.exp(dot_nn(keys[:low], q_b) - log)
                far_d = dot_nn(values[:low], g_b)
                inner = inner + col_sum(far * far_d)
            near_s = (near * (near_d - inner)).astype(BF)
            grad_q = dot_nn(k_t[:, low:end], near_s)
            gm32[low:end, HEAD_DIM : 2 * HEAD_DIM] = dot_nn(near_s, q_rows[low:end])
            gm32[low:end, 2 * HEAD_DIM :] = dot_nn(near.astype(BF), grad_rows[low:end])
            if b:
                far_s = (far * (far_d - inner)).astype(BF)
                grad_q = grad_q + dot_nn(k_t[:, :low], far_s)
                gm32[:low, HEAD_DIM : 2 * HEAD_DIM] += dot_nn(far_s, q_rows[low:end])
                gm32[:low, 2 * HEAD_DIM :] += dot_nn(far.astype(BF), grad_rows[low:end])
            gm32[low:end, :HEAD_DIM] = grad_q.T * HEAD_DIM ** (-0.5)
        for part in range(3):
            grad_mixed[:, part * wide + at : part * wide + at + HEAD_DIM] = gm32[
                :, part * HEAD_DIM : (part + 1) * HEAD_DIM
            ].astype(BF)
    bias_grad = col_sum(grad_mixed[...].astype(F32))
    gain_sum = jnp.zeros((1, x0.shape[1]), F32)
    shift_sum = gain_sum
    for i, x in enumerate((x0, x1, x2, x3)):
        back = dot_nt(grad_mixed[chunk_at(ids, i, rows), :], w_all[:, :wide3])
        hat, _ = normalise(x[...].astype(F32))
        gain_sum = gain_sum + col_sum(back * hat)
        shift_sum = shift_sum + col_sum(back)
        put_part(i, back, own, after_one, second)
    small[...] = jnp.zeros(small.shape, F32)
    small[0:1, :] = gain_sum
    small[1:2, :] = shift_sum
    small[2:6, :] = sums_two[0:4, :]
    small[pl.ds(6 + 2 * ids[3], 1), :wide3] = bias_grad
    small[pl.ds(7 + 2 * ids[3], 1), : up_bias.shape[1]] = up_bias[...]


def attn_grad_kernel(n_o, shard, ids, normed, grad_mixed, gh0, gh1, gh2, gh3, attended, *refs):
    outs, scratch = refs[:n_o], refs[n_o]
    wide3 = grad_mixed.shape[1]
    rows = gh0.shape[0]
    scratch[:, :wide3] = dot_tn(normed[...], grad_mixed[...])
    total = 0.0
    for i, gh in enumerate((gh0, gh1, gh2, gh3)):
        total = total + dot_tn(gh[...], attended[chunk_at(ids, i, rows), :])
    scratch[:, wide3:] = total
    emit_grad(ids, scratch, outs, shard)


def local(
    tokens,
    gain_one,
    shift_one,
    qkv_weight,
    qkv_bias,
    out_weight,
    out_bias,
    gain_two,
    shift_two,
    up_weight,
    up_bias,
    down_weight,
    down_bias,
    cotangent,
):
    plan = Plan()
    rows, width = tokens.shape
    shard = qkv_weight.shape[0]
    wide = qkv_weight.shape[2]
    wide3 = 3 * wide
    units = up_weight.shape[1]
    length = 4 * rows
    n_k = plan.n_k
    direct = n_k == 4 and shard % 16 == 0
    n_w = n_k if direct else 1
    n_o = n_k if direct else 1
    ids = jnp.stack([plan.k, plan.h, plan.r, plan.j]).astype(jnp.int32)
    row = lambda v: v.reshape(1, -1)
    row_gain_one, row_shift_one = row(gain_one), row(shift_one)
    row_gain_two, row_shift_two = row(gain_two), row(shift_two)

    def plane_pieces(value):
        if direct:
            return [value] + [plan.over_plane(value, p) for p in (1, 2, 3)]
        return [plan.ordered_weight(plan.plane_gather(value))[None]]

    def plane_got(pieces):
        return [plan.over_plane(pieces[p], p) for p in (1, 2, 3)] if direct else []

    def plane_total(pieces, got, *earlier):
        if direct:
            total = after(pieces[0], *earlier)
            for value in got:
                total = total + value.astype(F32)
            return total
        return plan.plane_sum(pieces[0].reshape((n_k, 2 * shard) + pieces[0].shape[1:]))

    def grad_outs(n):
        if direct:
            return [((2 * shard, n), F32)] + [((2 * shard, n), BF)] * (n_k - 1)
        return [((width, n), F32)]

    def parts():
        return [((rows, width), F32), ((rows, width), F32), ((2, rows, width), BF)]

    def toward_z(after_one, got_core):
        return (after_one + got_core[1].astype(F32)).astype(BF)

    x0 = plan.swap_home(tokens)
    attn_shard = jnp.concatenate([qkv_weight.reshape(shard, wide3), out_weight.T], 1)
    attn_spread = jnp.stack(plan.spread(attn_shard))
    biases = plan.to_slot(jnp.concatenate([qkv_bias.reshape(-1), up_bias]))
    qkv_bias_j, up_bias_j = row(biases[:wide3]), row(biases[wide3:])
    x1 = plan.over_z(x0)
    x2 = plan.over_core(x0)
    x3 = plan.over_core(x1)
    attn_w = plane_pieces(attn_spread)

    mlp_shard = jnp.concatenate([up_weight, down_weight.T], 1)
    mlp_spread = plan.spread(after(mlp_shard, attn_w[-1], x0))
    up_stack = jnp.stack([piece[:, :units] for piece in mlp_spread])
    down_stack = jnp.stack([piece[:, units:] for piece in mlp_spread])

    normed, mixed, w_all = call(
        lambda *refs: mixed_kernel(n_w, shard, *refs),
        [((length, width), BF), ((length, wide3), BF), ((width, width), BF)],
        [ids, x0, x1, x2, x3, row_gain_one, row_shift_one, qkv_bias_j] + attn_w,
        3,
        11,
    )
    g0 = plan.swap_home(after(cotangent, x1))
    up_pieces = plane_pieces(up_stack)

    attended, logs = call(
        attend_kernel,
        [((length, wide), BF), ((8, length), F32)],
        [ids, mixed],
        6,
        10,
    )
    out_t = jnp.stack([piece[..., wide3:] for piece in attn_w])
    out_z = plan.over_z(after(out_t, mixed))
    outs = [out_t, out_z, plan.over_core(out_t), plan.over_core(out_z)]
    att_z = plan.over_z(after(attended, g0, *up_pieces))
    down_pieces = plane_pieces(after(down_stack, attended))
    att_last = after(att_z, *outs, *down_pieces[1:])
    att = [attended, att_z, plan.over_core(attended), plan.over_core(att_last)]

    hidden_own, normed_two, act, slope, up_j = call(
        lambda *refs: forward_kernel(n_w, shard, *refs),
        [
            ((rows, width), F32),
            ((length, width), BF),
            ((length, units), BF),
            ((length, units), BF),
            ((width, units), BF),
        ],
        [ids]
        + att
        + outs
        + [x0, x1, x2, x3]
        + [row(out_bias), row_gain_two, row_shift_two, up_bias_j]
        + up_pieces,
        7,
        22,
        [pltpu.VMEM((4, width, wide), BF)],
    )
    g1 = plan.over_z(after(g0, att_z))
    gs = [g0, g1, plan.over_core(g0), plan.over_core(after(g1, slope))]
    grad_up, gn2_own, gn2_one, gn2_second, up_bias_grad, down_t = call(
        lambda *refs: backward_kernel(n_w, shard, *refs),
        [((length, units), BF)] + parts() + [((1, units), F32), ((width, units), BF)],
        [ids] + down_pieces + gs + [slope, up_j],
        5,
        18,
    )
    gn2_core = plan.over_core(gn2_second)
    gn2_z_in = toward_z(gn2_one, gn2_core)
    gn2_z = plan.over_z(gn2_z_in)
    out_own, out_one, out_second = call(
        mlp_out_kernel,
        parts(),
        [ids, act, down_t],
        2,
        12,
    )
    out_core = plan.over_core(out_second)
    out_z_in = toward_z(out_one, out_core)
    out_here = (hidden_own + out_own + out_core[0].astype(F32) + down_bias).astype(BF)
    mlp_grad = call(
        lambda *refs: mlp_grad_kernel(n_o, shard, *refs),
        grad_outs(2 * units),
        [ids, after(normed_two, gn2_z_in)] + gs + [act, grad_up],
        5,
        22,
        [pltpu.VMEM((width, 2 * units), F32)],
    )
    grad_hidden, gh0, sums_two = call(
        norm_two_kernel,
        [((rows, width), F32), ((rows, width), BF), ((8, width), F32)],
        [ids, gn2_own, gn2_core, gn2_z, after(hidden_own, mlp_grad[-1]), g0, row_gain_two],
        2,
        8,
    )
    gh1 = plan.over_z(gh0)
    mlp_got = plane_got(mlp_grad)
    ghs = [gh0, gh1, plan.over_core(gh0), plan.over_core(after(gh1, *mlp_got[:2]))]
    out_sent = [plan.swap_home(after(out_here, gh1)), plan.swap_next(after(out_z_in, gh1))]
    grad_mixed, gn1_own, gn1_one, gn1_second, small = call(
        attend_back_kernel,
        [((length, wide3), BF)] + parts() + [((16, width), F32)],
        [ids, after(mixed, out_z_in, out_here), logs, w_all]
        + ghs
        + [x0, x1, x2, x3, sums_two, up_bias_grad],
        12,
        22,
        [pltpu.VMEM((length, wide), F32), pltpu.VMEM((length, 3 * HEAD_DIM), F32)],
    )
    gn1_core = plan.over_core(after(gn1_second, *out_sent))
    gn1_z_in = toward_z(after(gn1_one, *mlp_got[2:]), gn1_core)
    gn1_z = plan.over_z(gn1_z_in)
    mlp_part = plane_total(mlp_grad, mlp_got, gn1_z_in).astype(BF).reshape(2, shard, 2 * units)
    mlp_summed = plan.unspread(mlp_part)
    attn_grad = call(
        lambda *refs: attn_grad_kernel(n_o, shard, *refs),
        grad_outs(width),
        [ids, after(normed, gn1_z_in), grad_mixed] + ghs + [attended],
        3,
        14,
        [pltpu.VMEM((width, width), F32)],
    )
    small = plan.chip_sum(after(small, gn1_z_in))
    (grad_low,) = call(
        norm_one_kernel,
        [((rows, width), BF)],
        [ids, gn1_own, gn1_core, gn1_z, after(x0, attn_grad[-1]), row_gain_one, grad_hidden],
        2,
        12,
    )
    home = plan.swap_home(grad_low)
    attn_grad = lax.optimization_barrier(tuple(attn_grad) + (small,))[:-1]
    attn_got = plane_got(attn_grad)

    attn_total = plane_total(attn_grad, attn_got, home)
    small = after(small, grad_low)
    small = small + plan.over_z(small)
    attn_part = after(attn_total, small).astype(BF).reshape(2, shard, width)
    small = small + plan.over_two(small)
    attn_summed = plan.unspread(attn_part)
    output = (out_sent[0].astype(F32) + out_sent[1].astype(F32)).astype(BF)
    grad_tokens = home.astype(F32)
    mine = lax.dynamic_slice_in_dim(small, 6 + 2 * plan.t, 2, 0)
    return (
        output,
        grad_tokens,
        small[0],
        small[1],
        attn_summed[:, :wide3].reshape(shard, 3, wide),
        mine[0, :wide3].reshape(3, wide),
        attn_summed[:, wide3:].T,
        small[2],
        small[3],
        small[4],
        mlp_summed[:, :units],
        mine[1, :units],
        mlp_summed[:, units:].T,
        small[5],
    )


def solution(mesh):
    in_specs = (
        P(("dp", "tensor"), None),
        P(),
        P(),
        P("dp", None, "tensor"),
        P(None, "tensor"),
        P("tensor", "dp"),
        P(),
        P(),
        P(),
        P("dp", "tensor"),
        P("tensor"),
        P("tensor", "dp"),
        P(),
        P(("dp", "tensor"), None),
    )
    out_specs = (
        P(("dp", "tensor"), None),
        P(("dp", "tensor"), None),
        P(),
        P(),
        P("dp", None, "tensor"),
        P(None, "tensor"),
        P("tensor", "dp"),
        P(),
        P(),
        P(),
        P("dp", "tensor"),
        P("tensor"),
        P("tensor", "dp"),
        P(),
    )
    return jax.shard_map(local, mesh=mesh, in_specs=in_specs, out_specs=out_specs, check_vma=False)
```
